128 devices in a mesh: grp: 4 (over x_lo, core), blk: 32 (over z, x_hi, y).
Axes of the slice: x: 4 (x_hi: 2, x_lo: 2; x = x_hi * 2 + x_lo), y: 4, z: 4, core: 2. Of those that a mesh axis runs over, the one named last changes fastest.
Arguments:
- head_vectors: float32 [32768, 256], P(('grp', 'blk')), may hold values from -6 to 6
- tail_vectors: float32 [32768, 256], P(('grp', 'blk')), may hold values from -6 to 6
- core_tensor: float32 [8192, 256], P(('grp', 'blk')), may hold values from -0.00390625 to 0.00390625
- core_moment: float32 [8192, 256], P(('grp', 'blk')), may hold values from -6 to 6
- core_second: float32 [8192, 256], P(('grp', 'blk')), may hold values from 0.5 to 2
- relation_table: float32 [1315, 32], replicated, may hold values from -6 to 6
- tile_relation: int32 [256, 8], P(('grp', 'blk')), may hold values from 0 to 1314
- positive_tail: int32 [32768, 4], P(('grp', 'blk')), may hold values from 0 to 255
- partner_table: int32 [32, 4, 4], P('blk'), may hold values from 0 to 3, as said below
Outputs:
- head_updated: float32 [32768, 256], P(('grp', 'blk'))
- tail_updated: float32 [32768, 256], P(('grp', 'blk'))
- head_losses: float32 [32768, 4], P(('grp', 'blk'))
- core_updated: float32 [8192, 256], P(('grp', 'blk'))
- moment_updated: float32 [8192, 256], P(('grp', 'blk'))
- second_updated: float32 [8192, 256], P(('grp', 'blk'))
- relation_grad: float32 [1315, 32], replicated
The draws below stay inside these ranges and needn't reach their ends.
Inputs may be any that keep to these rules, and one draw needn't show every extreme that they name: partner_table[b, 0, g] = g; for every b, each row and each column of partner_table[b] holds every number 0 to 3 once.
All inputs are finite; a program needn't handle non-finite values.
Results may differ from the reference program's by a relative error of at most 0.0077.
Values may be sent and summed in bfloat16 or wider, within the bound.
No kernel may reach another device: no remote copies, remote signals or barrier semaphores. Data moves between devices by JAX's collectives and lax.ppermute only.
A program may use at most 128 MiB of HBM per device.

```python
import math
import jax
import jax.numpy as jnp
from jax import lax

DE = 256
DR = 32
REL = 1315
TILE = 128
HEAD_DEV = 256
TAIL_DEV = 256
BUCKETS = 4
HEADS_ALL = 32768
TAILS_ALL = 32768
N_GRP = 4
N_BLK = 32


def draw_partner_table(key, part):
    block_keys = jax.random.split(jax.random.fold_in(key, 17), N_BLK)

    def one_block(block_key):
        coin_key, order_key = jax.random.split(block_key)
        offsets = jnp.concatenate([jnp.zeros((1,), jnp.int32), 1 + jax.random.permutation(order_key, BUCKETS - 1).astype(jnp.int32)])
        column = jnp.arange(BUCKETS, dtype=jnp.int32)
        cyclic = (column[None, :] + offsets[:, None]) % BUCKETS
        flipped = jnp.bitwise_xor(column[None, :], offsets[:, None])
        coin_flip = jax.random.randint(coin_key, (), 0, 2)
        return jnp.where(coin_flip == 1, flipped, cyclic).astype(jnp.int32)
    return jax.vmap(one_block)(block_keys)


def touch_ends(result, key, low, top_value):
    longest = result.shape.index(max(result.shape))
    spots = []
    for shift in (0, 1):
        where = [jax.random.randint(jax.random.fold_in(key, axis), (), 0, length) for axis, length in enumerate(result.shape)]
        where[longest] = (where[longest] + shift) % result.shape[longest]
        spots.append(tuple(where))
    return result.at[spots[0]].set(low).at[spots[1]].set(top_value)


def level_of(stream_key, extent, cuts, low, high):
    loudness = 1.0
    for axis_at, blocks in cuts:
        draws = jax.random.uniform(jax.random.fold_in(jax.random.fold_in(stream_key, 6), axis_at), (blocks,), jnp.float32, low / len(cuts), high / len(cuts))
        loudness = loudness * jnp.repeat(jnp.exp(draws), extent[axis_at] // blocks).reshape((-1,) + (1,) * (len(extent) - 1 - axis_at))
    return loudness


def gaussian(own_key, dims, spread, bound, cuts=(), kind=jnp.bfloat16):
    entries = spread * jax.random.normal(own_key, dims, jnp.float32)
    if cuts:
        entries = entries * level_of(own_key, dims, cuts, -0.22, 0.18)
    return jnp.clip(entries, -bound, bound).astype(kind)


def setup_inputs(seed: int = 0) -> dict:
    key_of = jax.random.split(jax.random.key(seed), 10)
    return {
        "head_vectors": gaussian(key_of[0], (HEADS_ALL, DE), 1.0, 6.0, ((0, 128),), jnp.float32),
        "tail_vectors": gaussian(key_of[1], (TAILS_ALL, DE), 1.0, 6.0, ((0, 128),), jnp.float32),
        "core_tensor": gaussian(key_of[2], (DE * DR, DE), (DE * DR * DE) ** -0.5, 0.00390625, ((0, 128),), jnp.float32),
        "core_moment": gaussian(key_of[3], (DE * DR, DE), 1.0, 6.0, ((0, 128),), jnp.float32),
        "core_second": jnp.clip(jnp.exp(math.log(2.0) - 1.3862944 * jax.random.uniform(key_of[4], (DE * DR, DE), jnp.float32) ** level_of(key_of[4], (DE * DR, DE), ((0, 128),), -0.2, 0.2)), 0.5, 2.0),
        "relation_table": gaussian(key_of[5], (REL, DR), 1.0, 6.0, (), jnp.float32),
        "tile_relation": touch_ends(jax.random.randint(key_of[6], (HEADS_ALL // TILE, BUCKETS * TAIL_DEV // TILE), 0, REL), jax.random.fold_in(key_of[6], 1), 0, REL - 1).astype(jnp.int32),
        "positive_tail": touch_ends(jax.random.randint(key_of[7], (HEADS_ALL, BUCKETS), 0, TAIL_DEV), jax.random.fold_in(key_of[7], 1), 0, TAIL_DEV - 1).astype(jnp.int32),
        "partner_table": draw_partner_table(jax.random.fold_in(key_of[9], 71), 0),
    }


entity_rate = 4.0
core_rate = 0.001
beta_first = 0.2
beta_second = 0.999

def train_pair(head_rows, tail_rows, core_low, relation_table, tile_ids, positive_col):
    head_count, width = head_rows.shape
    tail_count = tail_rows.shape[0]
    head_tiles = head_count // TILE
    tail_tiles = tail_count // TILE
    depth = core_low.shape[1] // width
    head_low = head_rows.astype(jnp.bfloat16)
    tail_low = tail_rows.astype(jnp.bfloat16)
    mixed_rows = jnp.dot(head_low, core_low, preferred_element_type=jnp.float32).astype(jnp.bfloat16)
    mixed_tiles = mixed_rows.reshape(head_tiles, TILE, depth, width)
    one_hot = (tile_ids.reshape(-1)[:, None] == jnp.arange(relation_table.shape[0], dtype=jnp.int32)[None, :]).astype(jnp.float32)
    rel_vectors = jnp.dot(one_hot, relation_table, precision=lax.Precision.HIGHEST).reshape(head_tiles, tail_tiles, depth).astype(jnp.bfloat16)
    rel_core = jnp.einsum('ihbc,ijb->ijhc', mixed_tiles.astype(jnp.float32), rel_vectors.astype(jnp.float32)).astype(jnp.bfloat16)
    tail_tiled = tail_low.reshape(tail_tiles, TILE, width)
    scores = jnp.einsum('ijhc,jtc->ihjt', rel_core.astype(jnp.float32), tail_tiled.astype(jnp.float32)).reshape(head_count, tail_count)
    is_positive = jnp.arange(tail_count, dtype=jnp.int32)[None, :] == positive_col[:, None]
    pair_loss = jnp.where(is_positive, jax.nn.softplus(-scores), jax.nn.softplus(scores) / tail_count)
    row_loss = lax.optimization_barrier(jnp.sum(pair_loss, axis=1))
    slope_low = jnp.where(is_positive, -jax.nn.sigmoid(-scores), jax.nn.sigmoid(scores) / tail_count).astype(jnp.bfloat16)
    slope_tiles = slope_low.reshape(head_tiles, TILE, tail_tiles, TILE).astype(jnp.float32)
    grad_relcore = jnp.einsum('ihjt,jtc->ijhc', slope_tiles, tail_tiled.astype(jnp.float32)).astype(jnp.bfloat16)
    grad_tail = jnp.einsum('ihjt,ijhc->jtc', slope_tiles, rel_core.astype(jnp.float32)).reshape(tail_count, width)
    grad_relvec = jnp.einsum('ijhc,ihbc->ijb', grad_relcore.astype(jnp.float32), mixed_tiles.astype(jnp.float32))
    grad_mixed = jnp.einsum('ijhc,ijb->ihbc', grad_relcore.astype(jnp.float32), rel_vectors.astype(jnp.float32)).reshape(head_count, depth * width).astype(jnp.bfloat16)
    grad_head = lax.dot_general(grad_mixed, core_low, (((1,), (1,)), ((), ())), preferred_element_type=jnp.float32)
    grad_core = lax.dot_general(head_low, grad_mixed, (((0,), (0,)), ((), ())), preferred_element_type=jnp.float32)
    grad_relation = jnp.dot(one_hot.T, grad_relvec.reshape(-1, depth), precision=lax.Precision.HIGHEST)
    return (head_rows - entity_rate * grad_head, tail_rows - entity_rate * grad_tail, grad_core, grad_relation, row_loss)

def reference(head_vectors, tail_vectors, core_tensor, core_moment, core_second, relation_table, tile_relation, positive_tail, partner_table):
    groups = N_GRP
    blocks = N_BLK
    head_tiles = HEAD_DEV // TILE
    tail_tiles = TAIL_DEV // TILE
    core_low = core_tensor.astype(jnp.bfloat16).reshape(DE, DR * DE)
    head_all = head_vectors.reshape(groups, blocks, HEAD_DEV, DE)
    tail_all = tail_vectors.reshape(groups, blocks, TAIL_DEV, DE)
    tile_all = tile_relation.reshape(groups, blocks, head_tiles, BUCKETS, tail_tiles)
    positive_all = positive_tail.reshape(groups, blocks, HEAD_DEV, BUCKETS)
    grad_total = jnp.zeros((DE, DR * DE), jnp.float32)
    relation_total = jnp.zeros((REL, DR), jnp.float32)
    loss_all = jnp.zeros((groups, blocks, HEAD_DEV, BUCKETS), jnp.float32)
    for round_index in range(BUCKETS):
        partition = jnp.transpose(partner_table[:, round_index, :]).astype(jnp.int32)

        def one_pair(carry, flat_index):
            member = flat_index // blocks
            block = flat_index % blocks
            chosen = partition[member, block]
            new_head, new_tail, grad_core, grad_relation, row_loss = train_pair(head_all[member, block], tail_all[chosen, block], core_low, relation_table, tile_all[member, block, :, chosen, :], positive_all[member, block, :, chosen])
            return ((carry[0] + grad_core, carry[1] + grad_relation), (new_head, new_tail, row_loss))
        (grad_total, relation_total), (head_stack, tail_stack, loss_stack) = lax.scan(one_pair, (grad_total, relation_total), jnp.arange(groups * blocks, dtype=jnp.int32))
        head_all = head_stack.reshape(groups, blocks, HEAD_DEV, DE)
        tail_stack = tail_stack.reshape(groups, blocks, TAIL_DEV, DE)
        matches = (partition[None, :, :] == jnp.arange(groups, dtype=jnp.int32)[:, None, None]).astype(jnp.int32)
        inverse = lax.optimization_barrier(jnp.sum(jnp.arange(groups, dtype=jnp.int32)[None, :, None] * matches, axis=1))
        tail_all = tail_stack[inverse, jnp.arange(blocks, dtype=jnp.int32)[None, :]]
        loss_all = loss_all.at[:, :, :, round_index].set(loss_stack.reshape(groups, blocks, HEAD_DEV))
    core_grad = grad_total.reshape(DE * DR, DE)
    normalized = core_grad / jnp.sqrt(jnp.mean(core_grad * core_grad) + 1e-06)
    moment_updated = beta_first * core_moment + (1.0 - beta_first) * normalized
    second_updated = beta_second * core_second + (1.0 - beta_second) * normalized * normalized
    core_updated = core_tensor - core_rate * moment_updated / (jnp.sqrt(second_updated) + 1e-08)
    return (head_all.reshape(-1, DE), tail_all.reshape(-1, DE), loss_all.reshape(-1, BUCKETS), core_updated, moment_updated, second_updated, relation_total)
```

```python
import jax
import jax.numpy as jnp
from jax import lax
from jax.experimental import pallas as pl
from jax.experimental.pallas import tpu as pltpu
from jax.sharding import Mesh, PartitionSpec as P

DE = 256
DR = 32
TILE = 128
GROUP = 4
PAIR_ROWS = 64
REL_PAD = 1408

entity_rate = 4.0
core_rate = 0.001
beta_first = 0.2
beta_second = 0.999

AXES = ("xl", "co", "z", "xh", "y")
MEMBERS = ("xl", "co")
GROUPS = ("z", "xh", "y")
CHIPS = ("xl", "z", "xh", "y")

f32 = jnp.float32
bf16 = jnp.bfloat16


def mm(a, b):
    return jnp.dot(a, b, preferred_element_type=f32)


def mm_nt(a, b):
    return lax.dot_general(a, b, (((1,), (1,)), ((), ())), preferred_element_type=f32)


def mm_tn(a, b):
    return lax.dot_general(a, b, (((0,), (0,)), ((), ())), preferred_element_type=f32)


def train_kernel(
    meta,
    mine,
    other,
    d0,
    d1,
    d2,
    d3,
    table,
    out_head,
    out_tail,
    out_loss,
    out_pay,
    rel_rows,
    id_rows,
    spread,
    spread_t,
    cores,
    grads,
    heads,
    heads_low,
    tails,
    tails_low,
    tail_grads,
):
    member = meta[0]
    co = meta[1]
    xl = meta[2]
    given = (d0, d1, d2, d3)

    for s in range(GROUP):
        for i in range(2):
            for t in range(GROUP):
                for j in range(2):
                    n = ((s * 2 + i) * GROUP + t) * 2 + j
                    rid = meta[19 + s * 16 + i * 8 + (t ^ member) * 2 + j]
                    rel_rows[n : n + 1, :] = table[pl.ds(rid, 1), :]
                    id_rows[n : n + 1, :] = jnp.full((1, 128), rid.astype(f32))

    rel_low = rel_rows[...].astype(bf16)
    copies = (
        lax.broadcasted_iota(jnp.int32, (DR, 256), 1) % DR
        == lax.broadcasted_iota(jnp.int32, (DR, 256), 0)
    ).astype(bf16)
    rel_wide = mm(rel_low, copies)
    on_row = (
        lax.broadcasted_iota(jnp.int32, (64, 8, 256), 2) // DR
        == lax.broadcasted_iota(jnp.int32, (64, 8, 256), 1)
    )
    spread_f = jnp.where(on_row, rel_wide[:, None, :], 0.0).reshape(512, 256)
    spread[...] = spread_f.astype(bf16)
    spread_t[...] = spread_f.T.astype(bf16)

    def core_step(q, carry):
        for src, side in ((mine, co), (other, 1 - co)):
            row = pl.multiple_of(q * 512, 512)
            parts = [
                mm(spread[...], src[pl.ds(row + 256 * e, 256), :]).reshape(64, 8, 256)
                for e in range(2)
            ]
            at = 64 * (2 * (q // 4) + side) + 16 * (q % 4)
            cores[:, pl.ds(pl.multiple_of(at, 16), 16), :] = jnp.concatenate(
                parts, axis=1
            ).astype(bf16)
        return carry

    lax.fori_loop(0, 8, core_step, 0)

    for s in range(GROUP):
        heads[s] = given[s][:, 0:256]
        tails[s] = given[s][:, 256:512]

    lane = lax.broadcasted_iota(jnp.int32, (TILE, TILE), 1)
    half = pl.multiple_of((member // 2) * 128, 128)
    odd = member % 2 == 1

    def round_step(k, carry):
        slots = [meta[3 + k * GROUP + (member ^ s)] ^ member for s in range(GROUP)]
        for s in range(GROUP):
            tails_low[s] = tails[slots[s]].astype(bf16)
            heads_low[s] = heads[s].astype(bf16)
        for s in range(GROUP):
            t = slots[s]
            own = meta[3 + k * GROUP + (member ^ s)]
            extra = given[s][:, 512:640]
            column = lax.broadcasted_iota(jnp.int32, (256, 128), 1) == own
            positive = jnp.sum(jnp.where(column, extra, 0.0), axis=1, keepdims=True).astype(
                jnp.int32
            )
            for i in range(2):
                rows = slice(TILE * i, TILE * i + TILE)
                head_low = heads_low[s, rows, :]
                head_part = heads_low[s, rows, pl.ds(half, 128)]
                grad_head = None
                row_loss = None
                for j in range(2):
                    cols = slice(TILE * j, TILE * j + TILE)
                    n = ((s * 2 + i) * GROUP + t) * 2 + j
                    core = cores[n]
                    tail_low = tails_low[s, cols, :]
                    rel_core = mm(head_low, core).astype(bf16)
                    score = mm_nt(rel_core, tail_low)
                    hit = lane + TILE * j == positive[rows]
                    signed = jnp.where(hit, -score, score)
                    slope = (
                        jax.nn.sigmoid(signed) * jnp.where(hit, -1.0, 1.0 / 256.0)
                    ).astype(bf16)
                    if s == 0:
                        part = jnp.sum(
                            (
                                jnp.maximum(signed, 0.0)
                                + jnp.log1p(jnp.exp(-jnp.abs(signed)))
                            )
                            * jnp.where(hit, 1.0, 1.0 / 256.0),
                            axis=1,
                            keepdims=True,
                        )
                        row_loss = part if row_loss is None else row_loss + part
                    grad_relcore = mm(slope, tail_low).astype(bf16)
                    grad_tail = mm_tn(slope, rel_core)
                    if i == 0:
                        tail_grads[s, cols, :] = grad_tail
                    else:
                        tail_grads[s, cols, :] += grad_tail
                    more = mm_nt(grad_relcore, core)
                    grad_head = more if grad_head is None else grad_head + more
                    outer = mm_tn(head_part, grad_relcore)
                    grads[n] = jnp.where(odd, outer[64:], outer[:64])
                heads[s, rows, :] -= entity_rate * grad_head
                if s == 0:
                    place = lax.broadcasted_iota(jnp.int32, (TILE, GROUP), 1) == k
                    out_loss[rows, :] = jnp.where(place, row_loss, out_loss[rows, :])
        for s in range(GROUP):
            tails[slots[s]] -= entity_rate * tail_grads[s]
        return carry

    out_loss[...] = jnp.zeros_like(out_loss)
    lax.fori_loop(0, GROUP, round_step, 0)
    out_head[...] = heads[0]
    out_tail[...] = tails[0]

    total = jnp.zeros((512, 256), f32)
    for e in range(8):
        low = grads[:, 8 * e : 8 * e + 8, :].reshape(512, 256).astype(bf16)
        part = mm(spread_t[...], low).astype(bf16)
        for d in range(4):
            out_pay[4 * e + d, 0:64, :] = part[64 * d : 64 * d + 64, :]
        own_core = mine[pl.ds(pl.multiple_of(xl * 2048 + 256 * e, 256), 256), :]
        total = total + mm_nt(low, own_core)
    wide = jnp.sum(jnp.where(on_row, total.reshape(64, 8, 256), 0.0), axis=1)
    folded = wide[:, :128] + wide[:, 128:]
    folded = folded + pltpu.roll(folded, 64, 1)
    folded = folded + pltpu.roll(folded, 32, 1)
    lanes = lax.broadcasted_iota(jnp.int32, (16, 128), 1)
    packed = jnp.zeros((16, 128), f32)
    names = jnp.zeros((16, 128), f32)
    for q in range(4):
        ids = id_rows[16 * q : 16 * q + 16, :]
        high = jnp.floor(ids * (1.0 / 256.0))
        rest = ids - 256.0 * high
        packed = jnp.where(lanes // 32 == q, folded[16 * q : 16 * q + 16, :], packed)
        names = jnp.where(lanes == 32 * q, high, jnp.where(lanes == 32 * q + 1, rest, names))
    tag = jnp.concatenate([packed, names], axis=1).astype(bf16)
    for d in range(32):
        out_pay[d, 64:80, :] = tag


def sum_kernel(got, out_grad, out_square, out_rel):
    total = got[0, 0:64, :].astype(f32)
    for d in range(1, 32):
        total = total + got[d, 0:64, :].astype(f32)
    out_grad[...] = total
    out_square[...] = jnp.full((128, 128), jnp.sum(total * total))
    tags = got[:, 64:80, :].reshape(512, 256)
    values = tags[:, :128]
    names = tags[:, 128:].astype(f32)
    for e in range(REL_PAD // 128):
        lane = (lax.broadcasted_iota(jnp.int32, (512, 128), 1) + 128 * e).astype(f32)
        out = jnp.zeros((DR, 128), f32)
        for q in range(4):
            rid = names[:, 32 * q : 32 * q + 1] * 256.0 + names[:, 32 * q + 1 : 32 * q + 2]
            hot = (lane == rid).astype(f32).astype(bf16)
            out = out + mm_tn(values, hot)[32 * q : 32 * q + 32, :]
        out_rel[:, 128 * e : 128 * e + 128] = out


def adam_kernel(
    squares, own, core, moment, second, r0, r1, r2, r3, out_core, out_moment, out_second, out_rel
):
    mean_square = jnp.sum(squares[...]) * (1.0 / 128.0 / (DE * DR * DE))
    scale = jnp.full((1, 1), mean_square) + 1e-06
    normalized = own[...] / jnp.sqrt(scale)
    moment_updated = beta_first * moment[...] + (1.0 - beta_first) * normalized
    second_updated = beta_second * second[...] + (1.0 - beta_second) * normalized * normalized
    out_moment[...] = moment_updated
    out_second[...] = second_updated
    out_core[...] = core[...] - core_rate * moment_updated / (jnp.sqrt(second_updated) + 1e-08)
    out_rel[...] = (r0[...] + r1[...]) + (r2[...] + r3[...])


def exchange(value, axes, step):
    size = lax.axis_size(axes)
    return lax.ppermute(value, axes, [(i, i ^ step) for i in range(size)])


def vmem(count):
    return [pl.BlockSpec(memory_space=pltpu.VMEM)] * count


def body(
    head_vectors,
    tail_vectors,
    core_tensor,
    core_moment,
    core_second,
    relation_table,
    tile_relation,
    positive_tail,
    partner_table,
):
    member = lax.axis_index(MEMBERS)
    co = lax.axis_index("co")
    xl = lax.axis_index("xl")
    rel_count = relation_table.shape[0]

    extra = jnp.zeros((256, 128), f32)
    extra = extra.at[:, 0:4].set(positive_tail.astype(f32))
    extra = extra.at[0:2, 8:16].set(tile_relation.astype(f32))
    own = jnp.concatenate([head_vectors, tail_vectors, extra], axis=1)
    group = [own] + [exchange(own, MEMBERS, s) for s in range(1, GROUP)]

    low = core_tensor.astype(bf16)
    mine = lax.all_to_all(
        jnp.broadcast_to(low[None], (64, 64, DE)), CHIPS, split_axis=0, concat_axis=0, tiled=True
    ).reshape(4096, DE)
    other = exchange(mine, "co", 1)

    ids = jnp.concatenate([g[0:2, 520:528].reshape(-1) for g in group]).astype(jnp.int32)
    meta = jnp.concatenate(
        [jnp.stack([member, co, xl]).astype(jnp.int32), partner_table.reshape(-1), ids]
    )
    head_now, tail_now, loss_now, pay = pl.pallas_call(
        train_kernel,
        out_shape=(
            jax.ShapeDtypeStruct((256, DE), f32),
            jax.ShapeDtypeStruct((256, DE), f32),
            jax.ShapeDtypeStruct((256, GROUP), f32),
            jax.ShapeDtypeStruct((32, 80, DE), bf16),
        ),
        in_specs=[pl.BlockSpec(memory_space=pltpu.SMEM)] + vmem(7),
        out_specs=tuple(vmem(4)),
        scratch_shapes=[
            pltpu.VMEM((64, DR), f32),
            pltpu.VMEM((64, 128), f32),
            pltpu.VMEM((512, 256), bf16),
            pltpu.VMEM((256, 512), bf16),
            pltpu.VMEM((64, 256, 256), bf16),
            pltpu.VMEM((64, 64, 256), f32),
            pltpu.VMEM((GROUP, 256, DE), f32),
            pltpu.VMEM((GROUP, 256, DE), bf16),
            pltpu.VMEM((GROUP, 256, DE), f32),
            pltpu.VMEM((GROUP, 256, DE), bf16),
            pltpu.VMEM((GROUP, 256, DE), f32),
        ],
        compiler_params=pltpu.CompilerParams(vmem_limit_bytes=48 * 1024 * 1024),
    )(meta, mine, other, *group, relation_table)

    got = lax.all_to_all(pay, GROUPS, split_axis=0, concat_axis=0, tiled=True)
    own_grad, square, rel_part = pl.pallas_call(
        sum_kernel,
        out_shape=(
            jax.ShapeDtypeStruct((64, DE), f32),
            jax.ShapeDtypeStruct((128, 128), f32),
            jax.ShapeDtypeStruct((DR, REL_PAD), f32),
        ),
        in_specs=vmem(1),
        out_specs=tuple(vmem(3)),
        compiler_params=pltpu.CompilerParams(vmem_limit_bytes=32 * 1024 * 1024),
    )(got)
    rel_parts = [rel_part] + [exchange(rel_part, MEMBERS, s) for s in range(1, GROUP)]
    squares = lax.all_to_all(square, AXES, split_axis=0, concat_axis=0, tiled=True)
    core_updated, moment_updated, second_updated, rel_sum = pl.pallas_call(
        adam_kernel,
        out_shape=(
            jax.ShapeDtypeStruct((64, DE), f32),
            jax.ShapeDtypeStruct((64, DE), f32),
            jax.ShapeDtypeStruct((64, DE), f32),
            jax.ShapeDtypeStruct((DR, REL_PAD), f32),
        ),
        in_specs=vmem(9),
        out_specs=tuple(vmem(4)),
        compiler_params=pltpu.CompilerParams(vmem_limit_bytes=32 * 1024 * 1024),
    )(squares, own_grad, core_tensor, core_moment, core_second, *rel_parts)
    return (
        head_now,
        tail_now,
        loss_now,
        core_updated,
        moment_updated,
        second_updated,
        rel_sum[:, :rel_count].T,
    )


def solution(mesh):
    fine = Mesh(mesh.devices.reshape(2, 2, 4, 2, 4), AXES)
    rows = P(AXES, None)
    return jax.shard_map(
        body,
        mesh=fine,
        in_specs=(rows, rows, rows, rows, rows, P(), rows, rows, P(GROUPS, None, None)),
        out_specs=(rows, rows, rows, rows, rows, rows, P()),
        check_vma=False,
    )
```

```python
import jax
import jax.numpy as jnp
from jax import lax
from jax.experimental import pallas as pl
from jax.experimental.pallas import tpu as pltpu
from jax.sharding import Mesh, PartitionSpec as P

DE = 256
DR = 32
TILE = 128
GROUP = 4
PAIR_ROWS = 64
REL_PAD = 1408
WHOLE = 60 * 1024 * 1024

entity_rate = 4.0
core_rate = 0.001
beta_first = 0.2
beta_second = 0.999

AXES = ("xl", "co", "z", "xh", "y")
MEMBERS = ("xl", "co")
GROUPS = ("z", "xh", "y")
CHIPS = ("xl", "z", "xh", "y")

f32 = jnp.float32
bf16 = jnp.bfloat16


def mm(a, b):
    return jnp.dot(a, b, preferred_element_type=f32)


def mm_nt(a, b):
    return lax.dot_general(a, b, (((1,), (1,)), ((), ())), preferred_element_type=f32)


def mm_tn(a, b):
    return lax.dot_general(a, b, (((0,), (0,)), ((), ())), preferred_element_type=f32)


def prepare_kernel(
    heads, tails, positive, tiles, core, out_own, out_core, hits, names, rows, wide, sems
):
    moves = [
        pltpu.make_async_copy(core, rows, sems.at[0]),
        pltpu.make_async_copy(tiles, names, sems.at[1]),
        pltpu.make_async_copy(positive, hits, sems.at[2]),
        pltpu.make_async_copy(heads, out_own.at[0:256, :], sems.at[3]),
        pltpu.make_async_copy(tails, out_own.at[256:512, :], sems.at[4]),
    ]
    for move in moves:
        move.start()
    moves[0].wait()
    low = rows[...].astype(bf16)
    for d in range(64):
        wide[d] = low
    spread_out = pltpu.make_async_copy(wide, out_core, sems.at[5])
    spread_out.start()
    pick = lax.broadcasted_iota(jnp.int32, (8, 8), 0) == lax.broadcasted_iota(
        jnp.int32, (8, 8), 1
    )
    out_own[512:544, :] = jnp.zeros((32, 256), f32)
    moves[1].wait()
    moves[2].wait()
    ids = names[...].astype(f32)
    out_own[512 : 512 + GROUP, :] = hits[...].astype(f32)
    for i in range(2):
        out_own[528 + 8 * i : 536 + 8 * i, 0:1] = jnp.sum(
            jnp.where(pick, ids[i : i + 1, :], 0.0), axis=1, keepdims=True
        )
    moves[3].wait()
    moves[4].wait()
    spread_out.wait()


def train_kernel(
    meta,
    mine,
    other,
    d0,
    d1,
    d2,
    d3,
    table,
    out_head,
    out_tail,
    out_loss,
    out_pay,
    table_low,
    spread,
    spread_t,
    cores,
    grads,
    heads,
    heads_low,
    heads_part,
    tails,
    tails_low,
    rel_core,
    grad_relcore,
    slopes,
    mine_here,
    other_here,
    sems,
):
    fetch_mine = pltpu.make_async_copy(mine, mine_here, sems.at[0])
    fetch_other = pltpu.make_async_copy(other, other_here, sems.at[1])
    fetch_mine.start()
    fetch_other.start()
    member = meta[0]
    co = meta[1]
    xl = meta[2]
    given = (d0, d1, d2, d3)
    rel_count = table.shape[1]

    table_low[...] = jnp.zeros_like(table_low)
    table_low[:, 0:rel_count] = table[...].astype(bf16)
    ids = jnp.concatenate([d[528:544, 0:1] for d in given], axis=0)
    hot = (
        ids == lax.broadcasted_iota(jnp.int32, (PAIR_ROWS, REL_PAD), 1).astype(f32)
    ).astype(f32).astype(bf16)
    rel_low = mm_nt(hot, table_low[...]).astype(bf16)
    copies = (
        lax.broadcasted_iota(jnp.int32, (DR, 256), 1) % DR
        == lax.broadcasted_iota(jnp.int32, (DR, 256), 0)
    ).astype(f32).astype(bf16)
    rel_wide = mm(rel_low, copies)
    on_row = (
        lax.broadcasted_iota(jnp.int32, (64, 8, 256), 2) // DR
        == lax.broadcasted_iota(jnp.int32, (64, 8, 256), 1)
    )
    spread_f = jnp.where(on_row, rel_wide[:, None, :], 0.0).reshape(512, 256)
    spread[...] = spread_f.astype(bf16)
    spread_t[...] = spread_f.T.astype(bf16)

    def core_step(src, side, q):
        row = pl.multiple_of(q * 512, 512)
        parts = [
            mm(spread[...], src[pl.ds(row + 256 * e, 256), :]).reshape(64, 8, 256)
            for e in range(2)
        ]
        at = 64 * (2 * (q // 4) + side) + 16 * (q % 4)
        cores[:, pl.ds(pl.multiple_of(at, 16), 16), :] = jnp.concatenate(parts, axis=1).astype(bf16)

    for fetch, src, side in ((fetch_mine, mine_here, co), (fetch_other, other_here, 1 - co)):
        fetch.wait()

        @pl.loop(0, 8, unroll=4)
        def _(q, src=src, side=side):
            core_step(src, side, q)

    for s in range(GROUP):
        heads[s] = given[s][0:256, :]
        tails[s] = given[s][256:512, :]

    row = lax.broadcasted_iota(jnp.int32, (TILE, 256), 0)
    half = pl.multiple_of((member // 2) * 128, 128)
    odd = member % 2 == 1

    def round_step(k, last):
        parts = [meta[3 + k * GROUP + (member ^ s)] for s in range(GROUP)]
        slots = range(GROUP)
        for s in slots:
            tails_low[s] = tails[parts[s] ^ member].astype(bf16)
            heads_low[s] = heads[s].astype(bf16)
            heads_part[s] = heads[s, :, pl.ds(half, 128)].T.astype(bf16)

        def at(s, i, j):
            return ((s * 2 + i) * GROUP + parts[s]) * 2 + j

        for s in slots:
            for i in range(2):
                rows = slice(TILE * i, TILE * i + TILE)
                for j in range(2):
                    rel_core[s, j, rows, :] = mm(heads_low[s, rows, :], cores[at(s, i, j)]).astype(
                        bf16
                    )
        for s in slots:
            positive = given[s][pl.ds(512 + parts[s], 1), :].astype(jnp.int32)
            row_loss = None
            for j in range(2):
                score = mm_nt(tails_low[s, TILE * j : TILE * j + TILE, :], rel_core[s, j])
                hit = row + TILE * j == positive
                signed = jnp.where(hit, -score, score)
                slopes[s, j] = (
                    jax.nn.sigmoid(signed) * jnp.where(hit, -1.0, 1.0 / 256.0)
                ).astype(bf16)
                if s == 0:
                    part = jnp.sum(
                        (jnp.maximum(signed, 0.0) + jnp.log1p(jnp.exp(-jnp.abs(signed))))
                        * jnp.where(hit, 1.0, 1.0 / 256.0),
                        axis=0,
                        keepdims=True,
                    )
                    row_loss = part if row_loss is None else row_loss + part
            if s == 0:
                line = lax.broadcasted_iota(jnp.int32, (GROUP, 256), 0) == k
                out_loss[...] = jnp.where(line, row_loss, out_loss[...])
        for s in slots:
            for j in range(2):
                cols = slice(TILE * j, TILE * j + TILE)
                grad_relcore[s, j] = mm_tn(slopes[s, j], tails_low[s, cols, :]).astype(bf16)
        for s in slots:
            for i in range(2):
                rows = slice(TILE * i, TILE * i + TILE)
                for j in range(2):
                    outer = mm(heads_part[s, :, rows], grad_relcore[s, j, rows, :])
                    grads[at(s, i, j)] = jnp.where(odd, outer[64:], outer[:64])
        for s in slots[:1] if last else slots:
            for i in range(2):
                rows = slice(TILE * i, TILE * i + TILE)
                grad_head = mm_nt(grad_relcore[s, 0, rows, :], cores[at(s, i, 0)])
                grad_head = grad_head + mm_nt(grad_relcore[s, 1, rows, :], cores[at(s, i, 1)])
                heads[s, rows, :] -= entity_rate * grad_head
        for s in slots:
            for j in range(2):
                cols = slice(TILE * j, TILE * j + TILE)
                tails[parts[s] ^ member, cols, :] -= entity_rate * mm(slopes[s, j], rel_core[s, j])

    out_loss[...] = jnp.zeros_like(out_loss)

    @pl.loop(0, GROUP - 1)
    def _(k):
        round_step(k, False)

    round_step(GROUP - 1, True)
    out_head[...] = heads[0]
    out_tail[...] = tails[0]

    total = jnp.zeros((512, 256), f32)
    for e in range(8):
        low = grads[:, 8 * e : 8 * e + 8, :].reshape(512, 256).astype(bf16)
        part = mm(spread_t[...], low).astype(bf16)
        for d in range(4):
            out_pay[4 * e + d, 0:64, :] = part[64 * d : 64 * d + 64, :]
        own_core = mine_here[pl.ds(pl.multiple_of(xl * 2048 + 256 * e, 256), 256), :]
        total = total + mm_nt(low, own_core)
    wide = jnp.sum(jnp.where(on_row, total.reshape(64, 8, 256), 0.0), axis=1)
    folded = wide[:, :128] + wide[:, 128:]
    folded = folded + pltpu.roll(folded, 64, 1)
    folded = folded + pltpu.roll(folded, 32, 1)
    lanes = lax.broadcasted_iota(jnp.int32, (16, 128), 1)
    packed = jnp.zeros((16, 128), f32)
    names = jnp.zeros((16, 128), f32)
    for q in range(4):
        own_ids = given[q][528:544, 0:1]
        high = jnp.floor(own_ids * (1.0 / 256.0))
        rest = own_ids - 256.0 * high
        packed = jnp.where(lanes // 32 == q, folded[16 * q : 16 * q + 16, :], packed)
        names = jnp.where(lanes == 32 * q, high, jnp.where(lanes == 32 * q + 1, rest, names))
    tag = jnp.concatenate([packed, names], axis=1).astype(bf16)
    for d in range(32):
        out_pay[d, 64:80, :] = tag


def sum_kernel(got, out_grad, out_square, out_rel):
    total = got[0, 0:64, :].astype(f32)
    for d in range(1, 32):
        total = total + got[d, 0:64, :].astype(f32)
    out_grad[...] = total
    out_square[...] = jnp.full((128, 128), jnp.sum(total * total))
    tags = got[:, 64:80, :].reshape(512, 256)
    values = tags[:, :128].astype(f32).T.astype(bf16)
    names = tags[:, 128:].astype(f32)
    for e in range(REL_PAD // 128):
        lane = (lax.broadcasted_iota(jnp.int32, (512, 128), 1) + 128 * e).astype(f32)
        out = jnp.zeros((DR, 128), f32)
        for q in range(4):
            rid = names[:, 32 * q : 32 * q + 1] * 256.0 + names[:, 32 * q + 1 : 32 * q + 2]
            hot = (lane == rid).astype(f32).astype(bf16)
            out = out + mm(values[32 * q : 32 * q + 32, :], hot)
        out_rel[:, 128 * e : 128 * e + 128] = out


def adam_kernel(
    squares, own, core, moment, second, r0, r1, r2, r3, out_core, out_moment, out_second, out_rel
):
    mean_square = jnp.sum(squares[...]) * (1.0 / 128.0 / (DE * DR * DE))
    scale = jnp.full((1, 1), mean_square) + 1e-06
    normalized = own[...] / jnp.sqrt(scale)
    moment_updated = beta_first * moment[...] + (1.0 - beta_first) * normalized
    second_updated = beta_second * second[...] + (1.0 - beta_second) * normalized * normalized
    out_moment[...] = moment_updated
    out_second[...] = second_updated
    out_core[...] = core[...] - core_rate * moment_updated / (jnp.sqrt(second_updated) + 1e-08)
    total = (r0[...] + r1[...]) + (r2[...] + r3[...])
    out_rel[...] = total[:, : out_rel.shape[1]]


def exchange(value, axes, step):
    size = lax.axis_size(axes)
    return lax.ppermute(value, axes, [(i, i ^ step) for i in range(size)])


def vmem(count):
    return [pl.BlockSpec(memory_space=pltpu.VMEM)] * count


def body(
    head_vectors,
    tail_vectors,
    core_tensor,
    core_moment,
    core_second,
    relation_table,
    tile_relation,
    positive_tail,
    partner_table,
):
    member = lax.axis_index(MEMBERS)
    co = lax.axis_index("co")
    xl = lax.axis_index("xl")
    rel_count = relation_table.shape[0]

    own, low = pl.pallas_call(
        prepare_kernel,
        out_shape=(
            jax.ShapeDtypeStruct((544, DE), f32),
            jax.ShapeDtypeStruct((64, 64, DE), bf16),
        ),
        in_specs=[pl.BlockSpec(memory_space=pl.ANY)] * 5,
        out_specs=(pl.BlockSpec(memory_space=pltpu.VMEM), pl.BlockSpec(memory_space=pl.ANY)),
        scratch_shapes=[
            pltpu.VMEM((GROUP, 256), jnp.int32),
            pltpu.VMEM((2, 8), jnp.int32),
            pltpu.VMEM((64, DE), f32),
            pltpu.VMEM((64, 64, DE), bf16),
            pltpu.SemaphoreType.DMA((6,)),
        ],
        compiler_params=pltpu.CompilerParams(vmem_limit_bytes=WHOLE),
    )(head_vectors, tail_vectors, positive_tail.T, tile_relation, core_tensor)
    across = exchange(own, "xl", 1)
    beside = exchange(own, "co", 1)

    mine = lax.all_to_all(low, CHIPS, split_axis=0, concat_axis=0, tiled=True).reshape(4096, DE)
    mine, across = lax.optimization_barrier((mine, across))
    other = exchange(mine, "co", 1)
    group = [own, beside, across, exchange(across, "co", 1)]

    meta = jnp.concatenate(
        [jnp.stack([member, co, xl]).astype(jnp.int32), partner_table.reshape(-1)]
    )
    head_now, tail_now, loss_now, pay = pl.pallas_call(
        train_kernel,
        out_shape=(
            jax.ShapeDtypeStruct((256, DE), f32),
            jax.ShapeDtypeStruct((256, DE), f32),
            jax.ShapeDtypeStruct((GROUP, 256), f32),
            jax.ShapeDtypeStruct((32, 80, DE), bf16),
        ),
        in_specs=[pl.BlockSpec(memory_space=pltpu.SMEM)]
        + [pl.BlockSpec(memory_space=pl.ANY)] * 2
        + vmem(5),
        out_specs=tuple(vmem(4)),
        scratch_shapes=[
            pltpu.VMEM((DR, REL_PAD), bf16),
            pltpu.VMEM((512, 256), bf16),
            pltpu.VMEM((256, 512), bf16),
            pltpu.VMEM((64, 256, 256), bf16),
            pltpu.VMEM((64, 64, 256), f32),
            pltpu.VMEM((GROUP, 256, DE), f32),
            pltpu.VMEM((GROUP, 256, DE), bf16),
            pltpu.VMEM((GROUP, 128, DE), bf16),
            pltpu.VMEM((GROUP, 256, DE), f32),
            pltpu.VMEM((GROUP, 256, DE), bf16),
            pltpu.VMEM((GROUP, 2, 256, DE), bf16),
            pltpu.VMEM((GROUP, 2, 256, DE), bf16),
            pltpu.VMEM((GROUP, 2, TILE, DE), bf16),
            pltpu.VMEM((4096, DE), bf16),
            pltpu.VMEM((4096, DE), bf16),
            pltpu.SemaphoreType.DMA((2,)),
        ],
        compiler_params=pltpu.CompilerParams(vmem_limit_bytes=48 * 1024 * 1024),
    )(meta, mine, other, *group, relation_table.T)

    got = lax.all_to_all(pay, GROUPS, split_axis=0, concat_axis=0, tiled=True)
    own_grad, square, rel_part = pl.pallas_call(
        sum_kernel,
        out_shape=(
            jax.ShapeDtypeStruct((64, DE), f32),
            jax.ShapeDtypeStruct((128, 128), f32),
            jax.ShapeDtypeStruct((DR, REL_PAD), f32),
        ),
        in_specs=vmem(1),
        out_specs=tuple(vmem(3)),
        compiler_params=pltpu.CompilerParams(vmem_limit_bytes=32 * 1024 * 1024),
    )(got)
    rel_parts = [rel_part] + [exchange(rel_part, MEMBERS, s) for s in range(1, GROUP)]
    squares = lax.all_to_all(square, AXES, split_axis=0, concat_axis=0, tiled=True)
    core_updated, moment_updated, second_updated, rel_sum = pl.pallas_call(
        adam_kernel,
        out_shape=(
            jax.ShapeDtypeStruct((64, DE), f32),
            jax.ShapeDtypeStruct((64, DE), f32),
            jax.ShapeDtypeStruct((64, DE), f32),
            jax.ShapeDtypeStruct((DR, rel_count), f32),
        ),
        in_specs=vmem(9),
        out_specs=tuple(vmem(4)),
        compiler_params=pltpu.CompilerParams(vmem_limit_bytes=32 * 1024 * 1024),
    )(squares, own_grad, core_tensor, core_moment, core_second, *rel_parts)
    return (
        head_now,
        tail_now,
        loss_now.T,
        core_updated,
        moment_updated,
        second_updated,
        rel_sum.T,
    )


def solution(mesh):
    fine = Mesh(mesh.devices.reshape(2, 2, 4, 2, 4), AXES)
    rows = P(AXES, None)
    return jax.shard_map(
        body,
        mesh=fine,
        in_specs=(rows, rows, rows, rows, rows, P(), rows, rows, P(GROUPS, None, None)),
        out_specs=(rows, rows, rows, rows, rows, rows, P()),
        check_vma=False,
    )
```

```python
import jax
import jax.numpy as jnp
from jax import lax
from jax.experimental import pallas as pl
from jax.experimental.pallas import tpu as pltpu
from jax.sharding import Mesh, PartitionSpec as P

DE = 256
DR = 32
TILE = 128
GROUP = 4
PAIR_ROWS = 64
REL_PAD = 1408
WHOLE = 60 * 1024 * 1024

entity_rate = 4.0
core_rate = 0.001
beta_first = 0.2
beta_second = 0.999

AXES = ("xl", "co", "z", "xh", "y")
MEMBERS = ("xl", "co")
GROUPS = ("z", "xh", "y")
CHIPS = ("xl", "z", "xh", "y")

f32 = jnp.float32
bf16 = jnp.bfloat16


def mm(a, b):
    return jnp.dot(a, b, preferred_element_type=f32)


def mm_nt(a, b):
    return lax.dot_general(a, b, (((1,), (1,)), ((), ())), preferred_element_type=f32)


def mm_tn(a, b):
    return lax.dot_general(a, b, (((0,), (0,)), ((), ())), preferred_element_type=f32)


def prepare_kernel(
    heads, tails, positive, tiles, core, out_own, out_core, hits, names, rows, both, wide, sems
):
    moves = [
        pltpu.make_async_copy(core, rows, sems.at[0]),
        pltpu.make_async_copy(heads, both.at[0:256, :], sems.at[1]),
        pltpu.make_async_copy(tails, both.at[256:512, :], sems.at[2]),
        pltpu.make_async_copy(tiles, names, sems.at[3]),
        pltpu.make_async_copy(positive, hits, sems.at[4]),
    ]
    for move in moves:
        move.start()
    moves[0].wait()
    low = rows[...].astype(bf16)
    for d in range(64):
        wide[d] = low
    spread_out = pltpu.make_async_copy(wide, out_core, sems.at[5])
    spread_out.start()
    for move in moves[1:]:
        move.wait()
    pick = lax.broadcasted_iota(jnp.int32, (8, 8), 0) == lax.broadcasted_iota(
        jnp.int32, (8, 8), 1
    )
    both[512:544, :] = jnp.zeros((32, 256), f32)
    both[512 : 512 + GROUP, :] = hits[...].astype(f32)
    ids = names[...].astype(f32)
    for i in range(2):
        column = jnp.sum(jnp.where(pick, ids[i : i + 1, :], 0.0), axis=1, keepdims=True)
        high = jnp.floor(column * (1.0 / 256.0))
        both[528 + 8 * i : 536 + 8 * i, 0:1] = high
        both[528 + 8 * i : 536 + 8 * i, 1:2] = column - 256.0 * high
    out_own[...] = both[...].astype(bf16)
    spread_out.wait()


def train_kernel(
    meta,
    mine,
    other,
    own_heads,
    own_tails,
    d0,
    d1,
    d2,
    d3,
    table,
    out_head,
    out_tail,
    out_loss,
    out_pay,
    table_low,
    spread,
    spread_t,
    cores,
    grads,
    heads,
    heads_low,
    heads_part,
    tails,
    tails_low,
    rel_core,
    grad_relcore,
    slopes,
    mine_here,
    other_here,
    sems,
):
    fetch_mine = pltpu.make_async_copy(mine, mine_here, sems.at[0])
    fetch_other = pltpu.make_async_copy(other, other_here, sems.at[1])
    fetch_mine.start()
    fetch_other.start()
    member = meta[0]
    co = meta[1]
    side = meta[2]
    given = (d0, d1, d2, d3)
    rel_count = table.shape[1]

    table_low[...] = jnp.zeros_like(table_low)
    table_low[:, 0:rel_count] = table[...].astype(bf16)
    names = [d[528:544, 0:128].astype(f32) for d in given]
    ids = jnp.concatenate([d[:, 0:1] * 256.0 + d[:, 1:2] for d in names], axis=0)
    hot = (
        ids == lax.broadcasted_iota(jnp.int32, (PAIR_ROWS, REL_PAD), 1).astype(f32)
    ).astype(f32).astype(bf16)
    rel_low = mm_nt(hot, table_low[...]).astype(bf16)
    copies = (
        lax.broadcasted_iota(jnp.int32, (DR, 256), 1) % DR
        == lax.broadcasted_iota(jnp.int32, (DR, 256), 0)
    ).astype(f32).astype(bf16)
    rel_wide = mm(rel_low, copies)
    on_row = (
        lax.broadcasted_iota(jnp.int32, (64, 8, 256), 2) // DR
        == lax.broadcasted_iota(jnp.int32, (64, 8, 256), 1)
    )
    spread_f = jnp.where(on_row, rel_wide[:, None, :], 0.0).reshape(512, 256)
    spread[...] = spread_f.astype(bf16)
    spread_t[...] = spread_f.T.astype(bf16)

    def core_step(src, core_of, q):
        row = pl.multiple_of(q * 512, 512)
        parts = [
            mm(spread[...], src[pl.ds(row + 256 * e, 256), :]).reshape(64, 8, 256)
            for e in range(2)
        ]
        at = 64 * (2 * (q // 4) + core_of) + 16 * (q % 4)
        cores[:, pl.ds(pl.multiple_of(at, 16), 16), :] = jnp.concatenate(parts, axis=1).astype(bf16)

    for fetch, src, core_of in ((fetch_mine, mine_here, co), (fetch_other, other_here, 1 - co)):
        fetch.wait()

        @pl.loop(0, 8, unroll=4)
        def _(q, src=src, core_of=core_of):
            core_step(src, core_of, q)

    heads[0] = own_heads[...]
    tails[0] = own_tails[...]
    for s in range(1, GROUP):
        heads[s] = given[s][0:256, :].astype(f32)
        tails[s] = given[s][256:512, :].astype(f32)
    which = lax.broadcasted_iota(jnp.int32, (16, 256), 0)

    row = lax.broadcasted_iota(jnp.int32, (TILE, 256), 0)
    near = pl.multiple_of(side * 128, 128)
    far = pl.multiple_of((1 - side) * 128, 128)
    even = (lax.broadcasted_iota(jnp.int32, (256, 128), 1) // 8) % 2 == 0

    def round_step(k, last):
        parts = [meta[3 + k * GROUP + (member ^ s)] for s in range(GROUP)]
        slots = range(GROUP)
        for s in slots:
            tails_low[s] = tails[parts[s] ^ member].astype(bf16)
            heads_low[s] = heads[s].astype(bf16)
            turned = jnp.where(even, heads[s, :, pl.ds(near, 128)], heads[s, :, pl.ds(far, 128)]).T
            heads_part[s] = jnp.where(co == 1, turned[64:], turned[:64]).astype(bf16)

        def at(s, i, j):
            return ((s * 2 + i) * GROUP + parts[s]) * 2 + j

        for s in slots:
            for i in range(2):
                rows = slice(TILE * i, TILE * i + TILE)
                for j in range(2):
                    rel_core[s, j, rows, :] = mm(heads_low[s, rows, :], cores[at(s, i, j)]).astype(
                        bf16
                    )
        for s in slots:
            positive = jnp.sum(
                jnp.where(which == parts[s], given[s][512:528, :].astype(f32), 0.0),
                axis=0,
                keepdims=True,
            ).astype(jnp.int32)
            row_loss = None
            for j in range(2):
                score = mm_nt(tails_low[s, TILE * j : TILE * j + TILE, :], rel_core[s, j])
                hit = row + TILE * j == positive
                signed = jnp.where(hit, -score, score)
                slopes[s, j] = (
                    jax.nn.sigmoid(signed) * jnp.where(hit, -1.0, 1.0 / 256.0)
                ).astype(bf16)
                if s == 0:
                    part = jnp.sum(
                        (jnp.maximum(signed, 0.0) + jnp.log1p(jnp.exp(-jnp.abs(signed))))
                        * jnp.where(hit, 1.0, 1.0 / 256.0),
                        axis=0,
                        keepdims=True,
                    )
                    row_loss = part if row_loss is None else row_loss + part
            if s == 0:
                line = lax.broadcasted_iota(jnp.int32, (GROUP, 256), 0) == k
                out_loss[...] = jnp.where(line, row_loss, out_loss[...])
        for s in slots:
            for j in range(2):
                cols = slice(TILE * j, TILE * j + TILE)
                grad_relcore[s, j] = mm_tn(slopes[s, j], tails_low[s, cols, :]).astype(bf16)
        for s in slots:
            for i in range(2):
                rows = slice(TILE * i, TILE * i + TILE)
                for j in range(2):
                    grads[at(s, i, j)] = mm(heads_part[s, :, rows], grad_relcore[s, j, rows, :])
        for s in slots[:1] if last else slots:
            for i in range(2):
                rows = slice(TILE * i, TILE * i + TILE)
                grad_head = mm_nt(grad_relcore[s, 0, rows, :], cores[at(s, i, 0)])
                grad_head = grad_head + mm_nt(grad_relcore[s, 1, rows, :], cores[at(s, i, 1)])
                heads[s, rows, :] -= entity_rate * grad_head
        for s in slots:
            for j in range(2):
                cols = slice(TILE * j, TILE * j + TILE)
                tails[parts[s] ^ member, cols, :] -= entity_rate * mm(slopes[s, j], rel_core[s, j])

    out_loss[...] = jnp.zeros_like(out_loss)

    @pl.loop(0, GROUP - 1)
    def _(k):
        round_step(k, False)

    round_step(GROUP - 1, True)
    out_head[...] = heads[0]
    out_tail[...] = tails[0]

    total = jnp.zeros((512, 256), f32)
    for e in range(8):
        low = grads[:, 8 * e : 8 * e + 8, :].reshape(512, 256).astype(bf16)
        part = mm(spread_t[...], low).astype(bf16)
        first = (side ^ (e % 2)) * 16 + (e // 2) * 4
        for d in range(4):
            out_pay[first + d, 0:64, :] = part[64 * d : 64 * d + 64, :]
        part_at = (side ^ (e % 2)) * 2048 + 256 * e
        own_core = mine_here[pl.ds(pl.multiple_of(part_at, 256), 256), :]
        total = total + mm_nt(low, own_core)
    wide = jnp.sum(jnp.where(on_row, total.reshape(64, 8, 256), 0.0), axis=1)
    folded = wide[:, :128] + wide[:, 128:]
    folded = folded + pltpu.roll(folded, 64, 1)
    folded = folded + pltpu.roll(folded, 32, 1)
    lanes = lax.broadcasted_iota(jnp.int32, (16, 128), 1)
    packed = jnp.zeros((16, 128), f32)
    tags = jnp.zeros((16, 128), f32)
    for q in range(4):
        high, rest = names[q][:, 0:1], names[q][:, 1:2]
        packed = jnp.where(lanes // 32 == q, folded[16 * q : 16 * q + 16, :], packed)
        tags = jnp.where(lanes == 32 * q, high, jnp.where(lanes == 32 * q + 1, rest, tags))
    tag = jnp.concatenate([packed, tags], axis=1).astype(bf16)
    for d in range(32):
        out_pay[d, 64:80, :] = tag


def sum_kernel(got, out_grad, out_square, out_rel):
    total = got[0, 0:64, :].astype(f32)
    for d in range(1, 32):
        total = total + got[d, 0:64, :].astype(f32)
    out_grad[...] = total
    out_square[...] = jnp.full((128, 128), jnp.sum(total * total))
    tags = got[:, 64:80, :].reshape(512, 256)
    values = tags[:, :128].astype(f32).T.astype(bf16)
    names = tags[:, 128:].astype(f32)
    for e in range(REL_PAD // 128):
        lane = (lax.broadcasted_iota(jnp.int32, (512, 128), 1) + 128 * e).astype(f32)
        out = jnp.zeros((DR, 128), f32)
        for q in range(4):
            rid = names[:, 32 * q : 32 * q + 1] * 256.0 + names[:, 32 * q + 1 : 32 * q + 2]
            hot = (lane == rid).astype(f32).astype(bf16)
            out = out + mm(values[32 * q : 32 * q + 32, :], hot)
        out_rel[:, 128 * e : 128 * e + 128] = out


def adam_kernel(
    squares, own, core, moment, second, r0, r1, r2, r3, out_core, out_moment, out_second, out_rel
):
    mean_square = jnp.sum(squares[...]) * (1.0 / 128.0 / (DE * DR * DE))
    scale = jnp.full((1, 1), mean_square) + 1e-06
    normalized = own[...] / jnp.sqrt(scale)
    moment_updated = beta_first * moment[...] + (1.0 - beta_first) * normalized
    second_updated = beta_second * second[...] + (1.0 - beta_second) * normalized * normalized
    out_moment[...] = moment_updated
    out_second[...] = second_updated
    out_core[...] = core[...] - core_rate * moment_updated / (jnp.sqrt(second_updated) + 1e-08)
    total = (r0[...] + r1[...]) + (r2[...] + r3[...])
    out_rel[...] = total[:, : out_rel.shape[1]]


def near_groups():
    return [
        [
            (((x * 2 + c) * 4 + z) * 2 + (x ^ w)) * 4 + y
            for x in range(2)
            for z in range(4)
            for y in range(4)
        ]
        for w in range(2)
        for c in range(2)
    ]


def exchange(value, axes, step):
    size = lax.axis_size(axes)
    return lax.ppermute(value, axes, [(i, i ^ step) for i in range(size)])


def vmem(count):
    return [pl.BlockSpec(memory_space=pltpu.VMEM)] * count


def body(
    head_vectors,
    tail_vectors,
    core_tensor,
    core_moment,
    core_second,
    relation_table,
    tile_relation,
    positive_tail,
    partner_table,
):
    member = lax.axis_index(MEMBERS)
    co = lax.axis_index("co")
    side = lax.axis_index("xl") ^ lax.axis_index("xh")
    rel_count = relation_table.shape[0]

    own, low = pl.pallas_call(
        prepare_kernel,
        out_shape=(
            jax.ShapeDtypeStruct((544, DE), bf16),
            jax.ShapeDtypeStruct((64, 64, DE), bf16),
        ),
        in_specs=[pl.BlockSpec(memory_space=pl.ANY)] * 5,
        out_specs=(pl.BlockSpec(memory_space=pltpu.VMEM), pl.BlockSpec(memory_space=pl.ANY)),
        scratch_shapes=[
            pltpu.VMEM((GROUP, 256), jnp.int32),
            pltpu.VMEM((2, 8), jnp.int32),
            pltpu.VMEM((64, DE), f32),
            pltpu.VMEM((544, DE), f32),
            pltpu.VMEM((64, 64, DE), bf16),
            pltpu.SemaphoreType.DMA((6,)),
        ],
        compiler_params=pltpu.CompilerParams(vmem_limit_bytes=WHOLE),
    )(head_vectors, tail_vectors, positive_tail.T, tile_relation, core_tensor)
    across = exchange(own, "xl", 1)
    beside = exchange(own, "co", 1)

    mine = lax.all_to_all(low, CHIPS, split_axis=0, concat_axis=0, tiled=True).reshape(4096, DE)
    mine, across = lax.optimization_barrier((mine, across))
    other = exchange(mine, "co", 1)
    group = [own, beside, across, exchange(across, "co", 1)]

    meta = jnp.concatenate(
        [jnp.stack([member, co, side]).astype(jnp.int32), partner_table.reshape(-1)]
    )
    head_now, tail_now, loss_now, pay = pl.pallas_call(
        train_kernel,
        out_shape=(
            jax.ShapeDtypeStruct((256, DE), f32),
            jax.ShapeDtypeStruct((256, DE), f32),
            jax.ShapeDtypeStruct((GROUP, 256), f32),
            jax.ShapeDtypeStruct((32, 80, DE), bf16),
        ),
        in_specs=[pl.BlockSpec(memory_space=pltpu.SMEM)]
        + [pl.BlockSpec(memory_space=pl.ANY)] * 2
        + vmem(7),
        out_specs=tuple(vmem(4)),
        scratch_shapes=[
            pltpu.VMEM((DR, REL_PAD), bf16),
            pltpu.VMEM((512, 256), bf16),
            pltpu.VMEM((256, 512), bf16),
            pltpu.VMEM((64, 256, 256), bf16),
            pltpu.VMEM((64, 64, 256), f32),
            pltpu.VMEM((GROUP, 256, DE), f32),
            pltpu.VMEM((GROUP, 256, DE), bf16),
            pltpu.VMEM((GROUP, 64, DE), bf16),
            pltpu.VMEM((GROUP, 256, DE), f32),
            pltpu.VMEM((GROUP, 256, DE), bf16),
            pltpu.VMEM((GROUP, 2, 256, DE), bf16),
            pltpu.VMEM((GROUP, 2, 256, DE), bf16),
            pltpu.VMEM((GROUP, 2, TILE, DE), bf16),
            pltpu.VMEM((4096, DE), bf16),
            pltpu.VMEM((4096, DE), bf16),
            pltpu.SemaphoreType.DMA((2,)),
        ],
        compiler_params=pltpu.CompilerParams(vmem_limit_bytes=48 * 1024 * 1024),
    )(meta, mine, other, head_vectors, tail_vectors, *group, relation_table.T)

    got = lax.all_to_all(
        pay, AXES, split_axis=0, concat_axis=0, tiled=True, axis_index_groups=near_groups()
    )
    own_grad, square, rel_part = pl.pallas_call(
        sum_kernel,
        out_shape=(
            jax.ShapeDtypeStruct((64, DE), f32),
            jax.ShapeDtypeStruct((128, 128), f32),
            jax.ShapeDtypeStruct((DR, REL_PAD), f32),
        ),
        in_specs=vmem(1),
        out_specs=tuple(vmem(3)),
        compiler_params=pltpu.CompilerParams(vmem_limit_bytes=32 * 1024 * 1024),
    )(got)
    rel_parts = [rel_part] + [exchange(rel_part, MEMBERS, s) for s in range(1, GROUP)]
    squares = lax.all_to_all(square, AXES, split_axis=0, concat_axis=0, tiled=True)
    core_updated, moment_updated, second_updated, rel_sum = pl.pallas_call(
        adam_kernel,
        out_shape=(
            jax.ShapeDtypeStruct((64, DE), f32),
            jax.ShapeDtypeStruct((64, DE), f32),
            jax.ShapeDtypeStruct((64, DE), f32),
            jax.ShapeDtypeStruct((DR, rel_count), f32),
        ),
        in_specs=vmem(9),
        out_specs=tuple(vmem(4)),
        compiler_params=pltpu.CompilerParams(vmem_limit_bytes=32 * 1024 * 1024),
    )(squares, own_grad, core_tensor, core_moment, core_second, *rel_parts)
    return (
        head_now,
        tail_now,
        loss_now.T,
        core_updated,
        moment_updated,
        second_updated,
        rel_sum.T,
    )


def solution(mesh):
    fine = Mesh(mesh.devices.reshape(2, 2, 4, 2, 4), AXES)
    rows = P(AXES, None)
    return jax.shard_map(
        body,
        mesh=fine,
        in_specs=(rows, rows, rows, rows, rows, P(), rows, rows, P(GROUPS, None, None)),
        out_specs=(rows, rows, rows, rows, rows, rows, P()),
        check_vma=False,
    )
```

```python
import jax
import jax.numpy as jnp
from jax import lax
from jax.experimental import pallas as pl
from jax.experimental.pallas import tpu as pltpu
from jax.sharding import Mesh, PartitionSpec as P

DE = 256
DR = 32
TILE = 128
GROUP = 4
PAIR_ROWS = 64
REL_PAD = 1408
WHOLE = 60 * 1024 * 1024
PREPARE = 60 * 1024 * 1024

entity_rate = 4.0
core_rate = 0.001
beta_first = 0.2
beta_second = 0.999

AXES = ("xl", "co", "z", "xh", "y")
MEMBERS = ("xl", "co")
GROUPS = ("z", "xh", "y")
CHIPS = ("xl", "z", "xh", "y")

f32 = jnp.float32
bf16 = jnp.bfloat16


def mm(a, b):
    return jnp.dot(a, b, preferred_element_type=f32)


def mm_nt(a, b):
    return lax.dot_general(a, b, (((1,), (1,)), ((), ())), preferred_element_type=f32)


def mm_tn(a, b):
    return lax.dot_general(a, b, (((0,), (0,)), ((), ())), preferred_element_type=f32)


def copies_kernel(core, out_core, rows, wide, sems):
    load = pltpu.make_async_copy(core, rows, sems.at[0])
    load.start()
    load.wait()
    low = rows[...].astype(bf16)
    moves = []
    for q in range(4):
        for d in range(16 * q, 16 * q + 16):
            wide[d] = low
        part = slice(16 * q, 16 * q + 16)
        moves.append(pltpu.make_async_copy(wide.at[part], out_core.at[part], sems.at[1 + q]))
        moves[-1].start()
    for move in moves:
        move.wait()


def prepare_kernel(heads, tails, positive, tiles, out_own, hits, names, both, sems):
    moves = [
        pltpu.make_async_copy(heads, both.at[0:256, :], sems.at[0]),
        pltpu.make_async_copy(tails, both.at[256:512, :], sems.at[1]),
        pltpu.make_async_copy(tiles, names, sems.at[2]),
        pltpu.make_async_copy(positive, hits, sems.at[3]),
    ]
    for move in moves:
        move.start()
    for move in moves:
        move.wait()
    pick = lax.broadcasted_iota(jnp.int32, (8, 8), 0) == lax.broadcasted_iota(
        jnp.int32, (8, 8), 1
    )
    both[512:544, :] = jnp.zeros((32, 256), f32)
    both[512 : 512 + GROUP, :] = hits[...].astype(f32)
    ids = names[...].astype(f32)
    for i in range(2):
        column = jnp.sum(jnp.where(pick, ids[i : i + 1, :], 0.0), axis=1, keepdims=True)
        high = jnp.floor(column * (1.0 / 256.0))
        both[528 + 8 * i : 536 + 8 * i, 0:1] = high
        both[528 + 8 * i : 536 + 8 * i, 1:2] = column - 256.0 * high
    out_own[...] = both[...].astype(bf16)


def on_rows():
    return (
        lax.broadcasted_iota(jnp.int32, (64, 8, 256), 2) // DR
        == lax.broadcasted_iota(jnp.int32, (64, 8, 256), 1)
    )


def core_step(spread, src, q):
    row = pl.multiple_of(q * 512, 512)
    parts = [
        mm(spread[...], src[pl.ds(row + 256 * e, 256), :]).reshape(64, 8, 256) for e in range(2)
    ]
    return jnp.concatenate(parts, axis=1).astype(bf16)


def form_kernel(mine, d0, d1, d2, d3, table, spread, spread_t, cores, table_low, marks, sems):
    rel_count = table.shape[1]
    moves = [
        pltpu.make_async_copy(d.at[528:544, :], marks.at[s], sems.at[s])
        for s, d in enumerate((d0, d1, d2, d3))
    ]
    for move in moves:
        move.start()
    table_low[...] = jnp.zeros_like(table_low)
    table_low[:, 0:rel_count] = table[...].astype(bf16)
    for move in moves:
        move.wait()
    names = marks[...].reshape(PAIR_ROWS, 256).astype(f32)
    ids = names[:, 0:1] * 256.0 + names[:, 1:2]
    hot = (
        ids == lax.broadcasted_iota(jnp.int32, (PAIR_ROWS, REL_PAD), 1).astype(f32)
    ).astype(f32).astype(bf16)
    rel_low = mm_nt(hot, table_low[...]).astype(bf16)
    copies = (
        lax.broadcasted_iota(jnp.int32, (DR, 256), 1) % DR
        == lax.broadcasted_iota(jnp.int32, (DR, 256), 0)
    ).astype(f32).astype(bf16)
    rel_wide = mm(rel_low, copies)
    on_row = on_rows()
    spread_f = jnp.where(on_row, rel_wide[:, None, :], 0.0).reshape(512, 256)
    spread[...] = spread_f.astype(bf16)
    spread_t[...] = spread_f.T.astype(bf16)

    @pl.loop(0, 8, unroll=4)
    def _(q):
        cores[:, pl.ds(pl.multiple_of(16 * q, 16), 16), :] = core_step(spread, mine, q)


def train_kernel(
    meta,
    mine,
    other,
    own_heads,
    own_tails,
    d0,
    d1,
    d2,
    d3,
    spread,
    spread_t,
    formed,
    out_head,
    out_tail,
    out_loss,
    out_pay,
    cores,
    grads,
    heads,
    heads_low,
    heads_part,
    tails,
    tails_low,
    rel_core,
    grad_relcore,
    slopes,
    other_here,
    gathered,
    sems,
):
    fetch_other = pltpu.make_async_copy(other, other_here, sems.at[GROUP])
    fetch_other.start()
    moves = [
        pltpu.make_async_copy(d, gathered.at[s], sems.at[s]) for s, d in enumerate((d0, d1, d2, d3))
    ]
    for move in moves:
        move.start()
    member = meta[0]
    co = meta[1]
    side = meta[2]
    given = [gathered.at[s] for s in range(GROUP)]
    on_row = on_rows()
    for x in range(2):
        at = pl.multiple_of(64 * (2 * x + co), 64)
        cores[:, pl.ds(at, 64), :] = formed[:, 64 * x : 64 * x + 64, :]
    fetch_other.wait()

    @pl.loop(0, 8, unroll=4)
    def _(q):
        at = 64 * (2 * (q // 4) + 1 - co) + 16 * (q % 4)
        cores[:, pl.ds(pl.multiple_of(at, 16), 16), :] = core_step(spread, other_here, q)

    for move in moves:
        move.wait()
    names = [d[528:544, 0:128].astype(f32) for d in given]
    heads[0] = own_heads[...]
    tails[0] = own_tails[...]
    for s in range(1, GROUP):
        heads[s] = given[s][0:256, :].astype(f32)
        tails[s] = given[s][256:512, :].astype(f32)
    which = lax.broadcasted_iota(jnp.int32, (16, 256), 0)

    row = lax.broadcasted_iota(jnp.int32, (TILE, 256), 0)
    near = pl.multiple_of(side * 128, 128)
    far = pl.multiple_of((1 - side) * 128, 128)
    even = (lax.broadcasted_iota(jnp.int32, (256, 128), 1) // 8) % 2 == 0

    def round_step(k, last):
        parts = [meta[3 + k * GROUP + (member ^ s)] for s in range(GROUP)]
        slots = range(GROUP)
        for s in slots:
            tails_low[s] = tails[parts[s] ^ member].astype(bf16)
            heads_low[s] = heads[s].astype(bf16)
            turned = jnp.where(even, heads[s, :, pl.ds(near, 128)], heads[s, :, pl.ds(far, 128)]).T
            heads_part[s] = jnp.where(co == 1, turned[64:], turned[:64]).astype(bf16)

        def at(s, i, j):
            return ((s * 2 + i) * GROUP + parts[s]) * 2 + j

        for s in slots:
            for i in range(2):
                rows = slice(TILE * i, TILE * i + TILE)
                for j in range(2):
                    rel_core[s, j, rows, :] = mm(heads_low[s, rows, :], cores[at(s, i, j)]).astype(
                        bf16
                    )
        for s in slots:
            positive = jnp.sum(
                jnp.where(which == parts[s], given[s][512:528, :].astype(f32), 0.0),
                axis=0,
                keepdims=True,
            ).astype(jnp.int32)
            row_loss = None
            for j in range(2):
                score = mm_nt(tails_low[s, TILE * j : TILE * j + TILE, :], rel_core[s, j])
                hit = row + TILE * j == positive
                signed = jnp.where(hit, -score, score)
                slopes[s, j] = (
                    jax.nn.sigmoid(signed) * jnp.where(hit, -1.0, 1.0 / 256.0)
                ).astype(bf16)
                if s == 0:
                    part = jnp.sum(
                        (jnp.maximum(signed, 0.0) + jnp.log1p(jnp.exp(-jnp.abs(signed))))
                        * jnp.where(hit, 1.0, 1.0 / 256.0),
                        axis=0,
                        keepdims=True,
                    )
                    row_loss = part if row_loss is None else row_loss + part
            if s == 0:
                line = lax.broadcasted_iota(jnp.int32, (GROUP, 256), 0) == k
                out_loss[...] = jnp.where(line, row_loss, out_loss[...])
        for s in slots:
            for j in range(2):
                cols = slice(TILE * j, TILE * j + TILE)
                grad_relcore[s, j] = mm_tn(slopes[s, j], tails_low[s, cols, :]).astype(bf16)
        for s in slots:
            for i in range(2):
                rows = slice(TILE * i, TILE * i + TILE)
                for j in range(2):
                    grads[at(s, i, j)] = mm(heads_part[s, :, rows], grad_relcore[s, j, rows, :])
        for s in slots[:1] if last else slots:
            for i in range(2):
                rows = slice(TILE * i, TILE * i + TILE)
                grad_head = mm_nt(grad_relcore[s, 0, rows, :], cores[at(s, i, 0)])
                grad_head = grad_head + mm_nt(grad_relcore[s, 1, rows, :], cores[at(s, i, 1)])
                heads[s, rows, :] -= entity_rate * grad_head
        for s in slots:
            for j in range(2):
                cols = slice(TILE * j, TILE * j + TILE)
                tails[parts[s] ^ member, cols, :] -= entity_rate * mm(slopes[s, j], rel_core[s, j])

    out_loss[...] = jnp.zeros_like(out_loss)

    @pl.loop(0, GROUP - 1)
    def _(k):
        round_step(k, False)

    round_step(GROUP - 1, True)
    out_head[...] = heads[0]
    out_tail[...] = tails[0]

    total = jnp.zeros((512, 256), f32)
    for e in range(8):
        low = grads[:, 8 * e : 8 * e + 8, :].reshape(512, 256).astype(bf16)
        part = mm(spread_t[...], low).astype(bf16)
        first = (side ^ (e % 2)) * 16 + (e // 2) * 4
        for d in range(4):
            out_pay[first + d, 0:64, :] = part[64 * d : 64 * d + 64, :]
        part_at = (side ^ (e % 2)) * 2048 + 256 * e
        own_core = mine[pl.ds(pl.multiple_of(part_at, 256), 256), :]
        total = total + mm_nt(low, own_core)
    wide = jnp.sum(jnp.where(on_row, total.reshape(64, 8, 256), 0.0), axis=1)
    folded = wide[:, :128] + wide[:, 128:]
    folded = folded + pltpu.roll(folded, 64, 1)
    folded = folded + pltpu.roll(folded, 32, 1)
    lanes = lax.broadcasted_iota(jnp.int32, (16, 128), 1)
    packed = jnp.zeros((16, 128), f32)
    tags = jnp.zeros((16, 128), f32)
    for q in range(4):
        high, rest = names[q][:, 0:1], names[q][:, 1:2]
        packed = jnp.where(lanes // 32 == q, folded[16 * q : 16 * q + 16, :], packed)
        tags = jnp.where(lanes == 32 * q, high, jnp.where(lanes == 32 * q + 1, rest, tags))
    tag = jnp.concatenate([packed, tags], axis=1).astype(bf16)
    for d in range(32):
        out_pay[d, 64:80, :] = tag


def sum_kernel(got, out_grad, out_square, out_rel):
    total = got[0, 0:64, :].astype(f32)
    for d in range(1, 32):
        total = total + got[d, 0:64, :].astype(f32)
    out_grad[...] = total
    out_square[...] = jnp.full((128, 128), jnp.sum(total * total))
    tags = got[:, 64:80, :].reshape(512, 256)
    values = tags[:, :128].astype(f32).T.astype(bf16)
    names = tags[:, 128:].astype(f32)
    for e in range(REL_PAD // 128):
        lane = (lax.broadcasted_iota(jnp.int32, (512, 128), 1) + 128 * e).astype(f32)
        out = jnp.zeros((DR, 128), f32)
        for q in range(4):
            rid = names[:, 32 * q : 32 * q + 1] * 256.0 + names[:, 32 * q + 1 : 32 * q + 2]
            hot = (lane == rid).astype(f32).astype(bf16)
            out = out + mm(values[32 * q : 32 * q + 32, :], hot)
        out_rel[:, 128 * e : 128 * e + 128] = out


def adam_kernel(
    squares, own, core, moment, second, r0, r1, r2, r3, out_core, out_moment, out_second, out_rel
):
    mean_square = jnp.sum(squares[...]) * (1.0 / 128.0 / (DE * DR * DE))
    scale = jnp.full((1, 1), mean_square) + 1e-06
    normalized = own[...] / jnp.sqrt(scale)
    moment_updated = beta_first * moment[...] + (1.0 - beta_first) * normalized
    second_updated = beta_second * second[...] + (1.0 - beta_second) * normalized * normalized
    out_moment[...] = moment_updated
    out_second[...] = second_updated
    out_core[...] = core[...] - core_rate * moment_updated / (jnp.sqrt(second_updated) + 1e-08)
    total = (r0[...] + r1[...]) + (r2[...] + r3[...])
    out_rel[...] = total[:, : out_rel.shape[1]]


def near_groups():
    return [
        [
            (((x * 2 + c) * 4 + z) * 2 + (x ^ w)) * 4 + y
            for x in range(2)
            for z in range(4)
            for y in range(4)
        ]
        for w in range(2)
        for c in range(2)
    ]


def exchange(value, axes, step):
    size = lax.axis_size(axes)
    return lax.ppermute(value, axes, [(i, i ^ step) for i in range(size)])


def vmem(count):
    return [pl.BlockSpec(memory_space=pltpu.VMEM)] * count


def body(
    head_vectors,
    tail_vectors,
    core_tensor,
    core_moment,
    core_second,
    relation_table,
    tile_relation,
    positive_tail,
    partner_table,
):
    member = lax.axis_index(MEMBERS)
    co = lax.axis_index("co")
    side = lax.axis_index("xl") ^ lax.axis_index("xh")
    rel_count = relation_table.shape[0]

    low = pl.pallas_call(
        copies_kernel,
        out_shape=jax.ShapeDtypeStruct((64, 64, DE), bf16),
        in_specs=[pl.BlockSpec(memory_space=pl.ANY)],
        out_specs=pl.BlockSpec(memory_space=pl.ANY),
        scratch_shapes=[
            pltpu.VMEM((64, DE), f32),
            pltpu.VMEM((64, 64, DE), bf16),
            pltpu.SemaphoreType.DMA((5,)),
        ],
        compiler_params=pltpu.CompilerParams(vmem_limit_bytes=WHOLE),
    )(core_tensor)
    own = pl.pallas_call(
        prepare_kernel,
        out_shape=jax.ShapeDtypeStruct((544, DE), bf16),
        in_specs=[pl.BlockSpec(memory_space=pl.ANY)] * 4,
        out_specs=pl.BlockSpec(memory_space=pltpu.VMEM),
        scratch_shapes=[
            pltpu.VMEM((GROUP, 256), jnp.int32),
            pltpu.VMEM((2, 8), jnp.int32),
            pltpu.VMEM((544, DE), f32),
            pltpu.SemaphoreType.DMA((4,)),
        ],
        compiler_params=pltpu.CompilerParams(vmem_limit_bytes=PREPARE),
        cost_estimate=pl.CostEstimate(
            flops=544 * 256, bytes_accessed=1024 * 1024, transcendentals=0
        ),
    )(head_vectors, tail_vectors, positive_tail.T, tile_relation)
    across = exchange(own, "xl", 1)
    beside = exchange(own, "co", 1)

    mine = lax.all_to_all(low, CHIPS, split_axis=0, concat_axis=0, tiled=True).reshape(4096, DE)
    beyond = exchange(across, "co", 1)
    mine, across, beside, beyond = lax.optimization_barrier((mine, across, beside, beyond))
    other = exchange(mine, "co", 1)
    group = [own, beside, across, beyond]
    spread, spread_t, formed = pl.pallas_call(
        form_kernel,
        out_shape=(
            jax.ShapeDtypeStruct((512, DE), bf16),
            jax.ShapeDtypeStruct((DE, 512), bf16),
            jax.ShapeDtypeStruct((PAIR_ROWS, 128, DE), bf16),
        ),
        in_specs=vmem(1) + [pl.BlockSpec(memory_space=pl.ANY)] * 4 + vmem(1),
        out_specs=tuple(vmem(3)),
        scratch_shapes=[
            pltpu.VMEM((DR, REL_PAD), bf16),
            pltpu.VMEM((GROUP, 16, DE), bf16),
            pltpu.SemaphoreType.DMA((GROUP,)),
        ],
        compiler_params=pltpu.CompilerParams(vmem_limit_bytes=24 * 1024 * 1024),
        cost_estimate=pl.CostEstimate(
            flops=2 * 512 * 256 * 4096, bytes_accessed=8 * 1024 * 1024, transcendentals=0
        ),
    )(mine, *group, relation_table.T)

    meta = jnp.concatenate(
        [jnp.stack([member, co, side]).astype(jnp.int32), partner_table.reshape(-1)]
    )
    head_now, tail_now, loss_now, pay = pl.pallas_call(
        train_kernel,
        out_shape=(
            jax.ShapeDtypeStruct((256, DE), f32),
            jax.ShapeDtypeStruct((256, DE), f32),
            jax.ShapeDtypeStruct((GROUP, 256), f32),
            jax.ShapeDtypeStruct((32, 80, DE), bf16),
        ),
        in_specs=[pl.BlockSpec(memory_space=pltpu.SMEM)]
        + vmem(1)
        + [pl.BlockSpec(memory_space=pl.ANY)]
        + vmem(2)
        + [pl.BlockSpec(memory_space=pl.ANY)] * 4
        + vmem(3),
        out_specs=tuple(vmem(4)),
        scratch_shapes=[
            pltpu.VMEM((64, 256, 256), bf16),
            pltpu.VMEM((64, 64, 256), f32),
            pltpu.VMEM((GROUP, 256, DE), f32),
            pltpu.VMEM((GROUP, 256, DE), bf16),
            pltpu.VMEM((GROUP, 64, DE), bf16),
            pltpu.VMEM((GROUP, 256, DE), f32),
            pltpu.VMEM((GROUP, 256, DE), bf16),
            pltpu.VMEM((GROUP, 2, 256, DE), bf16),
            pltpu.VMEM((GROUP, 2, 256, DE), bf16),
            pltpu.VMEM((GROUP, 2, TILE, DE), bf16),
            pltpu.VMEM((4096, DE), bf16),
            pltpu.VMEM((GROUP, 544, DE), bf16),
            pltpu.SemaphoreType.DMA((GROUP + 1,)),
        ],
        compiler_params=pltpu.CompilerParams(vmem_limit_bytes=36 * 1024 * 1024),
    )(meta, mine, other, head_vectors, tail_vectors, *group, spread, spread_t, formed)

    got = lax.all_to_all(
        pay, AXES, split_axis=0, concat_axis=0, tiled=True, axis_index_groups=near_groups()
    )
    own_grad, square, rel_part = pl.pallas_call(
        sum_kernel,
        out_shape=(
            jax.ShapeDtypeStruct((64, DE), f32),
            jax.ShapeDtypeStruct((128, 128), f32),
            jax.ShapeDtypeStruct((DR, REL_PAD), f32),
        ),
        in_specs=vmem(1),
        out_specs=tuple(vmem(3)),
        compiler_params=pltpu.CompilerParams(vmem_limit_bytes=32 * 1024 * 1024),
    )(got)
    rel_parts = [rel_part] + [exchange(rel_part, MEMBERS, s) for s in range(1, GROUP)]
    squares = lax.all_to_all(square, AXES, split_axis=0, concat_axis=0, tiled=True)
    core_updated, moment_updated, second_updated, rel_sum = pl.pallas_call(
        adam_kernel,
        out_shape=(
            jax.ShapeDtypeStruct((64, DE), f32),
            jax.ShapeDtypeStruct((64, DE), f32),
            jax.ShapeDtypeStruct((64, DE), f32),
            jax.ShapeDtypeStruct((DR, rel_count), f32),
        ),
        in_specs=vmem(9),
        out_specs=tuple(vmem(4)),
        compiler_params=pltpu.CompilerParams(vmem_limit_bytes=32 * 1024 * 1024),
    )(squares, own_grad, core_tensor, core_moment, core_second, *rel_parts)
    return (
        head_now,
        tail_now,
        loss_now.T,
        core_updated,
        moment_updated,
        second_updated,
        rel_sum.T,
    )


def solution(mesh):
    fine = Mesh(mesh.devices.reshape(2, 2, 4, 2, 4), AXES)
    rows = P(AXES, None)
    return jax.shard_map(
        body,
        mesh=fine,
        in_specs=(rows, rows, rows, rows, rows, P(), rows, rows, P(GROUPS, None, None)),
        out_specs=(rows, rows, rows, rows, rows, rows, P()),
        check_vma=False,
    )
```

```python
import jax
import jax.numpy as jnp
from jax import lax
from jax.experimental import pallas as pl
from jax.experimental.pallas import tpu as pltpu
from jax.sharding import Mesh, PartitionSpec as P

DE = 256
DR = 32
TILE = 128
GROUP = 4
PAIR_ROWS = 64
REL_PAD = 1408
WHOLE = 60 * 1024 * 1024
PREPARE = 60 * 1024 * 1024

entity_rate = 4.0
core_rate = 0.001
beta_first = 0.2
beta_second = 0.999

AXES = ("xl", "co", "z", "xh", "y")
MEMBERS = ("xl", "co")
GROUPS = ("z", "xh", "y")
CHIPS = ("xl", "z", "xh", "y")

f32 = jnp.float32
bf16 = jnp.bfloat16


def mm(a, b):
    return jnp.dot(a, b, preferred_element_type=f32)


def mm_nt(a, b):
    return lax.dot_general(a, b, (((1,), (1,)), ((), ())), preferred_element_type=f32)


def mm_tn(a, b):
    return lax.dot_general(a, b, (((0,), (0,)), ((), ())), preferred_element_type=f32)


def copies_kernel(core, out_core, rows, wide, sems):
    load = pltpu.make_async_copy(core, rows, sems.at[0])
    load.start()
    load.wait()
    low = rows[...].astype(bf16)
    moves = []
    for q in range(4):
        for d in range(16 * q, 16 * q + 16):
            wide[d] = low
        part = slice(16 * q, 16 * q + 16)
        moves.append(pltpu.make_async_copy(wide.at[part], out_core.at[part], sems.at[1 + q]))
        moves[-1].start()
    for move in moves:
        move.wait()


def prepare_kernel(
    heads, tails, positive, tiles, table, out_own, hits, names, both, rows, table_low, sems
):
    moves = [
        pltpu.make_async_copy(heads, both.at[0:256, :], sems.at[0]),
        pltpu.make_async_copy(tails, both.at[256:512, :], sems.at[1]),
        pltpu.make_async_copy(tiles, names, sems.at[2]),
        pltpu.make_async_copy(positive, hits, sems.at[3]),
        pltpu.make_async_copy(table, rows, sems.at[4]),
    ]
    for move in moves:
        move.start()
    for move in moves:
        move.wait()
    table_low[...] = jnp.zeros_like(table_low)
    table_low[:, 0 : rows.shape[1]] = rows[...].astype(bf16)
    pick = lax.broadcasted_iota(jnp.int32, (8, 8), 0) == lax.broadcasted_iota(
        jnp.int32, (8, 8), 1
    )
    both[512:544, :] = jnp.zeros((32, 256), f32)
    both[512 : 512 + GROUP, :] = hits[...].astype(f32)
    ids = names[...].astype(f32)
    for i in range(2):
        column = jnp.sum(jnp.where(pick, ids[i : i + 1, :], 0.0), axis=1, keepdims=True)
        high = jnp.floor(column * (1.0 / 256.0))
        both[528 + 8 * i : 536 + 8 * i, 0:1] = high
        both[528 + 8 * i : 536 + 8 * i, 1:2] = column - 256.0 * high
        hot = (
            column == lax.broadcasted_iota(jnp.int32, (8, REL_PAD), 1).astype(f32)
        ).astype(f32)
        hot = jnp.concatenate([hot, jnp.zeros_like(hot)], axis=0).astype(bf16)
        both[528 + 8 * i : 536 + 8 * i, 128 : 128 + DR] = mm_nt(hot, table_low[...])[0:8]
    out_own[...] = both[...].astype(bf16)


def on_rows():
    return (
        lax.broadcasted_iota(jnp.int32, (64, 8, 256), 2) // DR
        == lax.broadcasted_iota(jnp.int32, (64, 8, 256), 1)
    )


def core_step(spread, src, q):
    row = pl.multiple_of(q * 512, 512)
    parts = [
        mm(spread[...], src[pl.ds(row + 256 * e, 256), :]).reshape(64, 8, 256) for e in range(2)
    ]
    return jnp.concatenate(parts, axis=1).astype(bf16)


def form_kernel(mine, d0, d1, d2, d3, spread, spread_t, cores, marks, sems):
    moves = [
        pltpu.make_async_copy(d.at[528:544, :], marks.at[s], sems.at[s])
        for s, d in enumerate((d0, d1, d2, d3))
    ]
    for move in moves:
        move.start()
    for move in moves:
        move.wait()
    rel_low = marks[:, :, 128:256].reshape(PAIR_ROWS, 128)
    copies = (
        lax.broadcasted_iota(jnp.int32, (128, 256), 1) % DR
        == lax.broadcasted_iota(jnp.int32, (128, 256), 0)
    ).astype(f32).astype(bf16)
    rel_wide = mm(rel_low, copies)
    on_row = on_rows()
    spread_f = jnp.where(on_row, rel_wide[:, None, :], 0.0).reshape(512, 256)
    spread[...] = spread_f.astype(bf16)
    spread_t[...] = spread_f.T.astype(bf16)

    @pl.loop(0, 8, unroll=4)
    def _(q):
        cores[:, pl.ds(pl.multiple_of(16 * q, 16), 16), :] = core_step(spread, mine, q)


def train_kernel(
    meta,
    mine,
    other,
    own_heads,
    own_tails,
    d0,
    d1,
    d2,
    d3,
    spread,
    spread_t,
    formed,
    out_head,
    out_tail,
    out_loss,
    out_pay,
    cores,
    grads,
    heads,
    heads_low,
    heads_part,
    tails,
    tails_low,
    rel_core,
    grad_relcore,
    slopes,
    other_here,
    gathered,
    sems,
):
    fetch_other = pltpu.make_async_copy(other, other_here, sems.at[GROUP])
    fetch_other.start()
    moves = [
        pltpu.make_async_copy(d, gathered.at[s], sems.at[s]) for s, d in enumerate((d0, d1, d2, d3))
    ]
    for move in moves:
        move.start()
    member = meta[0]
    co = meta[1]
    side = meta[2]
    given = [gathered.at[s] for s in range(GROUP)]
    on_row = on_rows()
    for x in range(2):
        at = pl.multiple_of(64 * (2 * x + co), 64)
        cores[:, pl.ds(at, 64), :] = formed[:, 64 * x : 64 * x + 64, :]
    fetch_other.wait()

    @pl.loop(0, 8, unroll=4)
    def _(q):
        at = 64 * (2 * (q // 4) + 1 - co) + 16 * (q % 4)
        cores[:, pl.ds(pl.multiple_of(at, 16), 16), :] = core_step(spread, other_here, q)

    for move in moves:
        move.wait()
    names = [d[528:544, 0:128].astype(f32) for d in given]
    heads[0] = own_heads[...]
    tails[0] = own_tails[...]
    for s in range(1, GROUP):
        heads[s] = given[s][0:256, :].astype(f32)
        tails[s] = given[s][256:512, :].astype(f32)
    which = lax.broadcasted_iota(jnp.int32, (16, 256), 0)

    row = lax.broadcasted_iota(jnp.int32, (TILE, 256), 0)
    near = pl.multiple_of(side * 128, 128)
    far = pl.multiple_of((1 - side) * 128, 128)
    even = (lax.broadcasted_iota(jnp.int32, (256, 128), 1) // 8) % 2 == 0

    def round_step(k, last):
        parts = [meta[3 + k * GROUP + (member ^ s)] for s in range(GROUP)]
        slots = range(GROUP)
        for s in slots:
            tails_low[s] = tails[parts[s] ^ member].astype(bf16)
            heads_low[s] = heads[s].astype(bf16)
            turned = jnp.where(even, heads[s, :, pl.ds(near, 128)], heads[s, :, pl.ds(far, 128)]).T
            heads_part[s] = jnp.where(co == 1, turned[64:], turned[:64]).astype(bf16)

        def at(s, i, j):
            return ((s * 2 + i) * GROUP + parts[s]) * 2 + j

        for s in slots:
            for i in range(2):
                rows = slice(TILE * i, TILE * i + TILE)
                for j in range(2):
                    rel_core[s, j, rows, :] = mm(heads_low[s, rows, :], cores[at(s, i, j)]).astype(
                        bf16
                    )
        for s in slots:
            positive = jnp.sum(
                jnp.where(which == parts[s], given[s][512:528, :].astype(f32), 0.0),
                axis=0,
                keepdims=True,
            ).astype(jnp.int32)
            row_loss = None
            for j in range(2):
                score = mm_nt(tails_low[s, TILE * j : TILE * j + TILE, :], rel_core[s, j])
                hit = row + TILE * j == positive
                signed = jnp.where(hit, -score, score)
                slopes[s, j] = (
                    jax.nn.sigmoid(signed) * jnp.where(hit, -1.0, 1.0 / 256.0)
                ).astype(bf16)
                if s == 0:
                    part = jnp.sum(
                        (jnp.maximum(signed, 0.0) + jnp.log1p(jnp.exp(-jnp.abs(signed))))
                        * jnp.where(hit, 1.0, 1.0 / 256.0),
                        axis=0,
                        keepdims=True,
                    )
                    row_loss = part if row_loss is None else row_loss + part
            if s == 0:
                line = lax.broadcasted_iota(jnp.int32, (GROUP, 256), 0) == k
                out_loss[...] = jnp.where(line, row_loss, out_loss[...])
        for s in slots:
            for j in range(2):
                cols = slice(TILE * j, TILE * j + TILE)
                grad_relcore[s, j] = mm_tn(slopes[s, j], tails_low[s, cols, :]).astype(bf16)
        for s in slots:
            for i in range(2):
                rows = slice(TILE * i, TILE * i + TILE)
                for j in range(2):
                    grads[at(s, i, j)] = mm(heads_part[s, :, rows], grad_relcore[s, j, rows, :])
        for s in slots[:1] if last else slots:
            for i in range(2):
                rows = slice(TILE * i, TILE * i + TILE)
                grad_head = mm_nt(grad_relcore[s, 0, rows, :], cores[at(s, i, 0)])
                grad_head = grad_head + mm_nt(grad_relcore[s, 1, rows, :], cores[at(s, i, 1)])
                heads[s, rows, :] -= entity_rate * grad_head
        for s in slots:
            for j in range(2):
                cols = slice(TILE * j, TILE * j + TILE)
                tails[parts[s] ^ member, cols, :] -= entity_rate * mm(slopes[s, j], rel_core[s, j])

    out_loss[...] = jnp.zeros_like(out_loss)

    @pl.loop(0, GROUP - 1)
    def _(k):
        round_step(k, False)

    round_step(GROUP - 1, True)
    out_head[...] = heads[0]
    out_tail[...] = tails[0]

    total = jnp.zeros((512, 256), f32)
    for e in range(8):
        low = grads[:, 8 * e : 8 * e + 8, :].reshape(512, 256).astype(bf16)
        part = mm(spread_t[...], low).astype(bf16)
        first = (side ^ (e % 2)) * 16 + (e // 2) * 4
        for d in range(4):
            out_pay[first + d, 0:64, :] = part[64 * d : 64 * d + 64, :]
        part_at = (side ^ (e % 2)) * 2048 + 256 * e
        own_core = mine[pl.ds(pl.multiple_of(part_at, 256), 256), :]
        total = total + mm_nt(low, own_core)
    wide = jnp.sum(jnp.where(on_row, total.reshape(64, 8, 256), 0.0), axis=1)
    folded = wide[:, :128] + wide[:, 128:]
    folded = folded + pltpu.roll(folded, 64, 1)
    folded = folded + pltpu.roll(folded, 32, 1)
    lanes = lax.broadcasted_iota(jnp.int32, (16, 128), 1)
    packed = jnp.zeros((16, 128), f32)
    tags = jnp.zeros((16, 128), f32)
    for q in range(4):
        high, rest = names[q][:, 0:1], names[q][:, 1:2]
        packed = jnp.where(lanes // 32 == q, folded[16 * q : 16 * q + 16, :], packed)
        tags = jnp.where(lanes == 32 * q, high, jnp.where(lanes == 32 * q + 1, rest, tags))
    tag = jnp.concatenate([packed, tags], axis=1).astype(bf16)
    for d in range(32):
        out_pay[d, 64:80, :] = tag


def sum_kernel(got, out_grad, out_square, out_rel):
    total = got[0, 0:64, :].astype(f32)
    for d in range(1, 32):
        total = total + got[d, 0:64, :].astype(f32)
    out_grad[...] = total
    out_square[...] = jnp.full((128, 128), jnp.sum(total * total))
    tags = got[:, 64:80, :].reshape(512, 256)
    values = tags[:, :128].astype(f32).T.astype(bf16)
    names = tags[:, 128:].astype(f32)
    for e in range(REL_PAD // 128):
        lane = (lax.broadcasted_iota(jnp.int32, (512, 128), 1) + 128 * e).astype(f32)
        out = jnp.zeros((DR, 128), f32)
        for q in range(4):
            rid = names[:, 32 * q : 32 * q + 1] * 256.0 + names[:, 32 * q + 1 : 32 * q + 2]
            hot = (lane == rid).astype(f32).astype(bf16)
            out = out + mm(values[32 * q : 32 * q + 32, :], hot)
        out_rel[:, 128 * e : 128 * e + 128] = out


def adam_kernel(
    squares, own, core, moment, second, r0, r1, r2, r3, out_core, out_moment, out_second, out_rel
):
    mean_square = jnp.sum(squares[...]) * (1.0 / 128.0 / (DE * DR * DE))
    scale = jnp.full((1, 1), mean_square) + 1e-06
    normalized = own[...] / jnp.sqrt(scale)
    moment_updated = beta_first * moment[...] + (1.0 - beta_first) * normalized
    second_updated = beta_second * second[...] + (1.0 - beta_second) * normalized * normalized
    out_moment[...] = moment_updated
    out_second[...] = second_updated
    out_core[...] = core[...] - core_rate * moment_updated / (jnp.sqrt(second_updated) + 1e-08)
    total = (r0[...] + r1[...]) + (r2[...] + r3[...])
    out_rel[...] = total[:, : out_rel.shape[1]]


def near_groups():
    return [
        [
            (((x * 2 + c) * 4 + z) * 2 + (x ^ w)) * 4 + y
            for x in range(2)
            for z in range(4)
            for y in range(4)
        ]
        for w in range(2)
        for c in range(2)
    ]


def exchange(value, axes, step):
    size = lax.axis_size(axes)
    return lax.ppermute(value, axes, [(i, i ^ step) for i in range(size)])


def vmem(count):
    return [pl.BlockSpec(memory_space=pltpu.VMEM)] * count


def body(
    head_vectors,
    tail_vectors,
    core_tensor,
    core_moment,
    core_second,
    relation_table,
    tile_relation,
    positive_tail,
    partner_table,
):
    member = lax.axis_index(MEMBERS)
    co = lax.axis_index("co")
    side = lax.axis_index("xl") ^ lax.axis_index("xh")
    rel_count = relation_table.shape[0]

    low = pl.pallas_call(
        copies_kernel,
        out_shape=jax.ShapeDtypeStruct((64, 64, DE), bf16),
        in_specs=[pl.BlockSpec(memory_space=pl.ANY)],
        out_specs=pl.BlockSpec(memory_space=pl.ANY),
        scratch_shapes=[
            pltpu.VMEM((64, DE), f32),
            pltpu.VMEM((64, 64, DE), bf16),
            pltpu.SemaphoreType.DMA((5,)),
        ],
        compiler_params=pltpu.CompilerParams(vmem_limit_bytes=WHOLE),
    )(core_tensor)
    own = pl.pallas_call(
        prepare_kernel,
        out_shape=jax.ShapeDtypeStruct((544, DE), bf16),
        in_specs=[pl.BlockSpec(memory_space=pl.ANY)] * 5,
        out_specs=pl.BlockSpec(memory_space=pltpu.VMEM),
        scratch_shapes=[
            pltpu.VMEM((GROUP, 256), jnp.int32),
            pltpu.VMEM((2, 8), jnp.int32),
            pltpu.VMEM((544, DE), f32),
            pltpu.VMEM((DR, rel_count), f32),
            pltpu.VMEM((DR, REL_PAD), bf16),
            pltpu.SemaphoreType.DMA((5,)),
        ],
        compiler_params=pltpu.CompilerParams(vmem_limit_bytes=PREPARE),
        cost_estimate=pl.CostEstimate(
            flops=544 * 256, bytes_accessed=1024 * 1024, transcendentals=0
        ),
    )(head_vectors, tail_vectors, positive_tail.T, tile_relation, relation_table.T)
    across = exchange(own, "xl", 1)
    beside = exchange(own, "co", 1)

    mine = lax.all_to_all(low, CHIPS, split_axis=0, concat_axis=0, tiled=True).reshape(4096, DE)
    beyond = exchange(across, "co", 1)
    mine, across, beside, beyond = lax.optimization_barrier((mine, across, beside, beyond))
    other = exchange(mine, "co", 1)
    group = [own, beside, across, beyond]
    spread, spread_t, formed = pl.pallas_call(
        form_kernel,
        out_shape=(
            jax.ShapeDtypeStruct((512, DE), bf16),
            jax.ShapeDtypeStruct((DE, 512), bf16),
            jax.ShapeDtypeStruct((PAIR_ROWS, 128, DE), bf16),
        ),
        in_specs=vmem(1) + [pl.BlockSpec(memory_space=pl.ANY)] * 4,
        out_specs=tuple(vmem(3)),
        scratch_shapes=[
            pltpu.VMEM((GROUP, 16, DE), bf16),
            pltpu.SemaphoreType.DMA((GROUP,)),
        ],
        compiler_params=pltpu.CompilerParams(vmem_limit_bytes=24 * 1024 * 1024),
        cost_estimate=pl.CostEstimate(
            flops=2 * 512 * 256 * 4096, bytes_accessed=8 * 1024 * 1024, transcendentals=0
        ),
    )(mine, *group)

    meta = jnp.concatenate(
        [jnp.stack([member, co, side]).astype(jnp.int32), partner_table.reshape(-1)]
    )
    head_now, tail_now, loss_now, pay = pl.pallas_call(
        train_kernel,
        out_shape=(
            jax.ShapeDtypeStruct((256, DE), f32),
            jax.ShapeDtypeStruct((256, DE), f32),
            jax.ShapeDtypeStruct((GROUP, 256), f32),
            jax.ShapeDtypeStruct((32, 80, DE), bf16),
        ),
        in_specs=[pl.BlockSpec(memory_space=pltpu.SMEM)]
        + vmem(1)
        + [pl.BlockSpec(memory_space=pl.ANY)]
        + vmem(2)
        + [pl.BlockSpec(memory_space=pl.ANY)] * 4
        + vmem(3),
        out_specs=tuple(vmem(4)),
        scratch_shapes=[
            pltpu.VMEM((64, 256, 256), bf16),
            pltpu.VMEM((64, 64, 256), f32),
            pltpu.VMEM((GROUP, 256, DE), f32),
            pltpu.VMEM((GROUP, 256, DE), bf16),
            pltpu.VMEM((GROUP, 64, DE), bf16),
            pltpu.VMEM((GROUP, 256, DE), f32),
            pltpu.VMEM((GROUP, 256, DE), bf16),
            pltpu.VMEM((GROUP, 2, 256, DE), bf16),
            pltpu.VMEM((GROUP, 2, 256, DE), bf16),
            pltpu.VMEM((GROUP, 2, TILE, DE), bf16),
            pltpu.VMEM((4096, DE), bf16),
            pltpu.VMEM((GROUP, 544, DE), bf16),
            pltpu.SemaphoreType.DMA((GROUP + 1,)),
        ],
        compiler_params=pltpu.CompilerParams(vmem_limit_bytes=36 * 1024 * 1024),
    )(meta, mine, other, head_vectors, tail_vectors, *group, spread, spread_t, formed)

    got = lax.all_to_all(
        pay, AXES, split_axis=0, concat_axis=0, tiled=True, axis_index_groups=near_groups()
    )
    own_grad, square, rel_part = pl.pallas_call(
        sum_kernel,
        out_shape=(
            jax.ShapeDtypeStruct((64, DE), f32),
            jax.ShapeDtypeStruct((128, 128), f32),
            jax.ShapeDtypeStruct((DR, REL_PAD), f32),
        ),
        in_specs=vmem(1),
        out_specs=tuple(vmem(3)),
        compiler_params=pltpu.CompilerParams(vmem_limit_bytes=32 * 1024 * 1024),
    )(got)
    rel_parts = [rel_part] + [exchange(rel_part, MEMBERS, s) for s in range(1, GROUP)]
    squares = lax.all_to_all(square, AXES, split_axis=0, concat_axis=0, tiled=True)
    core_updated, moment_updated, second_updated, rel_sum = pl.pallas_call(
        adam_kernel,
        out_shape=(
            jax.ShapeDtypeStruct((64, DE), f32),
            jax.ShapeDtypeStruct((64, DE), f32),
            jax.ShapeDtypeStruct((64, DE), f32),
            jax.ShapeDtypeStruct((DR, rel_count), f32),
        ),
        in_specs=vmem(9),
        out_specs=tuple(vmem(4)),
        compiler_params=pltpu.CompilerParams(vmem_limit_bytes=32 * 1024 * 1024),
    )(squares, own_grad, core_tensor, core_moment, core_second, *rel_parts)
    return (
        head_now,
        tail_now,
        loss_now.T,
        core_updated,
        moment_updated,
        second_updated,
        rel_sum.T,
    )


def solution(mesh):
    fine = Mesh(mesh.devices.reshape(2, 2, 4, 2, 4), AXES)
    rows = P(AXES, None)
    return jax.shard_map(
        body,
        mesh=fine,
        in_specs=(rows, rows, rows, rows, rows, P(), rows, rows, P(GROUPS, None, None)),
        out_specs=(rows, rows, rows, rows, rows, rows, P()),
        check_vma=False,
    )
```

```python
import jax
import jax.numpy as jnp
from jax import lax
from jax.experimental import pallas as pl
from jax.experimental.pallas import tpu as pltpu
from jax.sharding import Mesh, PartitionSpec as P

DE = 256
DR = 32
TILE = 128
GROUP = 4
PAIR_ROWS = 64
REL_PAD = 1408
WHOLE = 60 * 1024 * 1024
PREPARE = 60 * 1024 * 1024

entity_rate = 4.0
core_rate = 0.001
beta_first = 0.2
beta_second = 0.999

AXES = ("xl", "co", "z", "xh", "y")
MEMBERS = ("xl", "co")
GROUPS = ("z", "xh", "y")
CHIPS = ("xl", "z", "xh", "y")

f32 = jnp.float32
bf16 = jnp.bfloat16


def mm(a, b):
    return jnp.dot(a, b, preferred_element_type=f32)


def mm_nt(a, b):
    return lax.dot_general(a, b, (((1,), (1,)), ((), ())), preferred_element_type=f32)


def mm_tn(a, b):
    return lax.dot_general(a, b, (((0,), (0,)), ((), ())), preferred_element_type=f32)


def copies_kernel(core, out_core, rows, wide, sems):
    load = pltpu.make_async_copy(core, rows, sems.at[0])
    load.start()
    load.wait()
    low = rows[...].astype(bf16)
    moves = []
    for q in range(4):
        for d in range(16 * q, 16 * q + 16):
            wide[d] = low
        part = slice(16 * q, 16 * q + 16)
        moves.append(pltpu.make_async_copy(wide.at[part], out_core.at[part], sems.at[1 + q]))
        moves[-1].start()
    for move in moves:
        move.wait()


def prepare_kernel(
    heads, tails, positive, tiles, table, out_own, hits, names, both, rows, table_low, sems
):
    moves = [
        pltpu.make_async_copy(heads, both.at[0:256, :], sems.at[0]),
        pltpu.make_async_copy(tails, both.at[256:512, :], sems.at[1]),
        pltpu.make_async_copy(tiles, names, sems.at[2]),
        pltpu.make_async_copy(positive, hits, sems.at[3]),
        pltpu.make_async_copy(table, rows, sems.at[4]),
    ]
    for move in moves:
        move.start()
    for move in moves:
        move.wait()
    table_low[...] = jnp.zeros_like(table_low)
    table_low[:, 0 : rows.shape[1]] = rows[...].astype(bf16)
    pick = lax.broadcasted_iota(jnp.int32, (8, 8), 0) == lax.broadcasted_iota(
        jnp.int32, (8, 8), 1
    )
    both[512:544, :] = jnp.zeros((32, 256), f32)
    both[512 : 512 + GROUP, :] = hits[...].astype(f32)
    ids = names[...].astype(f32)
    for i in range(2):
        column = jnp.sum(jnp.where(pick, ids[i : i + 1, :], 0.0), axis=1, keepdims=True)
        high = jnp.floor(column * (1.0 / 256.0))
        both[528 + 8 * i : 536 + 8 * i, 0:1] = high
        both[528 + 8 * i : 536 + 8 * i, 1:2] = column - 256.0 * high
        hot = (
            column == lax.broadcasted_iota(jnp.int32, (8, REL_PAD), 1).astype(f32)
        ).astype(f32)
        hot = jnp.concatenate([hot, jnp.zeros_like(hot)], axis=0).astype(bf16)
        both[528 + 8 * i : 536 + 8 * i, 128 : 128 + DR] = mm_nt(hot, table_low[...])[0:8]
    out_own[...] = both[...].astype(bf16)


def on_rows():
    return (
        lax.broadcasted_iota(jnp.int32, (64, 8, 256), 2) // DR
        == lax.broadcasted_iota(jnp.int32, (64, 8, 256), 1)
    )


def core_step(spread, src, q):
    row = pl.multiple_of(q * 512, 512)
    parts = [
        mm(spread[...], src[pl.ds(row + 256 * e, 256), :]).reshape(64, 8, 256) for e in range(2)
    ]
    return jnp.concatenate(parts, axis=1).astype(bf16)


def form_kernel(mine, d0, d1, d2, d3, spread, spread_t, cores, marks, sems):
    moves = [
        pltpu.make_async_copy(d.at[528:544, :], marks.at[s], sems.at[s])
        for s, d in enumerate((d0, d1, d2, d3))
    ]
    for move in moves:
        move.start()
    for move in moves:
        move.wait()
    rel_low = marks[:, :, 128:256].reshape(PAIR_ROWS, 128)
    copies = (
        lax.broadcasted_iota(jnp.int32, (128, 256), 1) % DR
        == lax.broadcasted_iota(jnp.int32, (128, 256), 0)
    ).astype(f32).astype(bf16)
    rel_wide = mm(rel_low, copies)
    on_row = on_rows()
    spread_f = jnp.where(on_row, rel_wide[:, None, :], 0.0).reshape(512, 256)
    spread[...] = spread_f.astype(bf16)
    spread_t[...] = spread_f.T.astype(bf16)

    @pl.loop(0, 8, unroll=8)
    def _(q):
        cores[:, pl.ds(pl.multiple_of(16 * q, 16), 16), :] = core_step(spread, mine, q)


def train_kernel(
    meta,
    mine,
    other,
    own_heads,
    own_tails,
    d0,
    d1,
    d2,
    d3,
    spread,
    spread_t,
    formed,
    out_head,
    out_tail,
    out_loss,
    out_pay,
    cores,
    grads,
    heads,
    heads_low,
    heads_part,
    tails,
    tails_low,
    rel_core,
    grad_relcore,
    slopes,
    other_here,
    gathered,
    sems,
):
    fetch_other = pltpu.make_async_copy(other, other_here, sems.at[GROUP])
    fetch_other.start()
    moves = [
        pltpu.make_async_copy(d, gathered.at[s], sems.at[s]) for s, d in enumerate((d0, d1, d2, d3))
    ]
    for move in moves:
        move.start()
    member = meta[0]
    co = meta[1]
    side = meta[2]
    given = [gathered.at[s] for s in range(GROUP)]
    on_row = on_rows()
    for x in range(2):
        at = pl.multiple_of(64 * (2 * x + co), 64)
        cores[:, pl.ds(at, 64), :] = formed[:, 64 * x : 64 * x + 64, :]
    fetch_other.wait()

    @pl.loop(0, 8, unroll=8)
    def _(q):
        at = 64 * (2 * (q // 4) + 1 - co) + 16 * (q % 4)
        cores[:, pl.ds(pl.multiple_of(at, 16), 16), :] = core_step(spread, other_here, q)

    for move in moves:
        move.wait()
    names = [d[528:544, 0:128].astype(f32) for d in given]
    heads[0] = own_heads[...]
    tails[0] = own_tails[...]
    for s in range(1, GROUP):
        heads[s] = given[s][0:256, :].astype(f32)
        tails[s] = given[s][256:512, :].astype(f32)
    which = lax.broadcasted_iota(jnp.int32, (16, 256), 0)

    row = lax.broadcasted_iota(jnp.int32, (TILE, 256), 0)
    near = pl.multiple_of(side * 128, 128)
    far = pl.multiple_of((1 - side) * 128, 128)
    even = (lax.broadcasted_iota(jnp.int32, (256, 128), 1) // 8) % 2 == 0

    def round_step(k, last):
        parts = [meta[3 + k * GROUP + (member ^ s)] for s in range(GROUP)]
        slots = range(GROUP)
        for s in slots:
            tails_low[s] = tails[parts[s] ^ member].astype(bf16)
            heads_low[s] = heads[s].astype(bf16)
            turned = jnp.where(even, heads[s, :, pl.ds(near, 128)], heads[s, :, pl.ds(far, 128)]).T
            heads_part[s] = jnp.where(co == 1, turned[64:], turned[:64]).astype(bf16)

        def at(s, i, j):
            return ((s * 2 + i) * GROUP + parts[s]) * 2 + j

        for s in slots:
            for i in range(2):
                rows = slice(TILE * i, TILE * i + TILE)
                for j in range(2):
                    rel_core[s, j, rows, :] = mm(heads_low[s, rows, :], cores[at(s, i, j)]).astype(
                        bf16
                    )
        for s in slots:
            positive = jnp.sum(
                jnp.where(which == parts[s], given[s][512:528, :].astype(f32), 0.0),
                axis=0,
                keepdims=True,
            ).astype(jnp.int32)
            row_loss = None
            for j in range(2):
                score = mm_nt(tails_low[s, TILE * j : TILE * j + TILE, :], rel_core[s, j])
                hit = row + TILE * j == positive
                signed = jnp.where(hit, -score, score)
                slopes[s, j] = (
                    jax.nn.sigmoid(signed) * jnp.where(hit, -1.0, 1.0 / 256.0)
                ).astype(bf16)
                if s == 0:
                    part = jnp.sum(
                        (jnp.maximum(signed, 0.0) + jnp.log1p(jnp.exp(-jnp.abs(signed))))
                        * jnp.where(hit, 1.0, 1.0 / 256.0),
                        axis=0,
                        keepdims=True,
                    )
                    row_loss = part if row_loss is None else row_loss + part
            if s == 0:
                line = lax.broadcasted_iota(jnp.int32, (GROUP, 256), 0) == k
                out_loss[...] = jnp.where(line, row_loss, out_loss[...])
        for s in slots:
            for j in range(2):
                cols = slice(TILE * j, TILE * j + TILE)
                grad_relcore[s, j] = mm_tn(slopes[s, j], tails_low[s, cols, :]).astype(bf16)
        for s in slots:
            for i in range(2):
                rows = slice(TILE * i, TILE * i + TILE)
                for j in range(2):
                    grads[at(s, i, j)] = mm(heads_part[s, :, rows], grad_relcore[s, j, rows, :])
        for s in slots[:1] if last else slots:
            for i in range(2):
                rows = slice(TILE * i, TILE * i + TILE)
                grad_head = mm_nt(grad_relcore[s, 0, rows, :], cores[at(s, i, 0)])
                grad_head = grad_head + mm_nt(grad_relcore[s, 1, rows, :], cores[at(s, i, 1)])
                heads[s, rows, :] -= entity_rate * grad_head
        for s in slots:
            for j in range(2):
                cols = slice(TILE * j, TILE * j + TILE)
                tails[parts[s] ^ member, cols, :] -= entity_rate * mm(slopes[s, j], rel_core[s, j])

    out_loss[...] = jnp.zeros_like(out_loss)

    @pl.loop(0, GROUP - 1)
    def _(k):
        round_step(k, False)

    round_step(GROUP - 1, True)
    out_head[...] = heads[0]
    out_tail[...] = tails[0]

    total = jnp.zeros((512, 256), f32)
    for e in range(8):
        low = grads[:, 8 * e : 8 * e + 8, :].reshape(512, 256).astype(bf16)
        part = mm(spread_t[...], low).astype(bf16)
        first = (side ^ (e % 2)) * 16 + (e // 2) * 4
        for d in range(4):
            out_pay[first + d, 0:64, :] = part[64 * d : 64 * d + 64, :]
        part_at = (side ^ (e % 2)) * 2048 + 256 * e
        own_core = mine[pl.ds(pl.multiple_of(part_at, 256), 256), :]
        total = total + mm_nt(low, own_core)
    wide = jnp.sum(jnp.where(on_row, total.reshape(64, 8, 256), 0.0), axis=1)
    folded = wide[:, :128] + wide[:, 128:]
    folded = folded + pltpu.roll(folded, 64, 1)
    folded = folded + pltpu.roll(folded, 32, 1)
    lanes = lax.broadcasted_iota(jnp.int32, (16, 128), 1)
    packed = jnp.zeros((16, 128), f32)
    tags = jnp.zeros((16, 128), f32)
    for q in range(4):
        high, rest = names[q][:, 0:1], names[q][:, 1:2]
        packed = jnp.where(lanes // 32 == q, folded[16 * q : 16 * q + 16, :], packed)
        tags = jnp.where(lanes == 32 * q, high, jnp.where(lanes == 32 * q + 1, rest, tags))
    tag = jnp.concatenate([packed, tags], axis=1).astype(bf16)
    for d in range(32):
        out_pay[d, 64:80, :] = tag


def sum_kernel(got, out_grad, out_square, out_rel):
    total = got[0, 0:64, :].astype(f32)
    for d in range(1, 32):
        total = total + got[d, 0:64, :].astype(f32)
    out_grad[...] = total
    out_square[...] = jnp.full((128, 128), jnp.sum(total * total))
    tags = got[:, 64:80, :].reshape(512, 256)
    values = tags[:, :128].astype(f32).T.astype(bf16)
    names = tags[:, 128:].astype(f32)
    for e in range(REL_PAD // 128):
        lane = (lax.broadcasted_iota(jnp.int32, (512, 128), 1) + 128 * e).astype(f32)
        out = jnp.zeros((DR, 128), f32)
        for q in range(4):
            rid = names[:, 32 * q : 32 * q + 1] * 256.0 + names[:, 32 * q + 1 : 32 * q + 2]
            hot = (lane == rid).astype(f32).astype(bf16)
            out = out + mm(values[32 * q : 32 * q + 32, :], hot)
        out_rel[:, 128 * e : 128 * e + 128] = out


def adam_kernel(
    squares, own, core, moment, second, r0, r1, r2, r3, out_core, out_moment, out_second, out_rel
):
    mean_square = jnp.sum(squares[...]) * (1.0 / 128.0 / (DE * DR * DE))
    scale = jnp.full((1, 1), mean_square) + 1e-06
    normalized = own[...] / jnp.sqrt(scale)
    moment_updated = beta_first * moment[...] + (1.0 - beta_first) * normalized
    second_updated = beta_second * second[...] + (1.0 - beta_second) * normalized * normalized
    out_moment[...] = moment_updated
    out_second[...] = second_updated
    out_core[...] = core[...] - core_rate * moment_updated / (jnp.sqrt(second_updated) + 1e-08)
    total = (r0[...] + r1[...]) + (r2[...] + r3[...])
    out_rel[...] = total[:, : out_rel.shape[1]]


def near_groups():
    return [
        [
            (((x * 2 + c) * 4 + z) * 2 + (x ^ w)) * 4 + y
            for x in range(2)
            for z in range(4)
            for y in range(4)
        ]
        for w in range(2)
        for c in range(2)
    ]


def exchange(value, axes, step):
    size = lax.axis_size(axes)
    return lax.ppermute(value, axes, [(i, i ^ step) for i in range(size)])


def vmem(count):
    return [pl.BlockSpec(memory_space=pltpu.VMEM)] * count


def body(
    head_vectors,
    tail_vectors,
    core_tensor,
    core_moment,
    core_second,
    relation_table,
    tile_relation,
    positive_tail,
    partner_table,
):
    member = lax.axis_index(MEMBERS)
    co = lax.axis_index("co")
    side = lax.axis_index("xl") ^ lax.axis_index("xh")
    rel_count = relation_table.shape[0]

    low = pl.pallas_call(
        copies_kernel,
        out_shape=jax.ShapeDtypeStruct((64, 64, DE), bf16),
        in_specs=[pl.BlockSpec(memory_space=pl.ANY)],
        out_specs=pl.BlockSpec(memory_space=pl.ANY),
        scratch_shapes=[
            pltpu.VMEM((64, DE), f32),
            pltpu.VMEM((64, 64, DE), bf16),
            pltpu.SemaphoreType.DMA((5,)),
        ],
        compiler_params=pltpu.CompilerParams(vmem_limit_bytes=WHOLE),
    )(core_tensor)
    own = pl.pallas_call(
        prepare_kernel,
        out_shape=jax.ShapeDtypeStruct((544, DE), bf16),
        in_specs=[pl.BlockSpec(memory_space=pl.ANY)] * 5,
        out_specs=pl.BlockSpec(memory_space=pltpu.VMEM),
        scratch_shapes=[
            pltpu.VMEM((GROUP, 256), jnp.int32),
            pltpu.VMEM((2, 8), jnp.int32),
            pltpu.VMEM((544, DE), f32),
            pltpu.VMEM((DR, rel_count), f32),
            pltpu.VMEM((DR, REL_PAD), bf16),
            pltpu.SemaphoreType.DMA((5,)),
        ],
        compiler_params=pltpu.CompilerParams(vmem_limit_bytes=PREPARE),
        cost_estimate=pl.CostEstimate(
            flops=544 * 256, bytes_accessed=1024 * 1024, transcendentals=0
        ),
    )(head_vectors, tail_vectors, positive_tail.T, tile_relation, relation_table.T)
    across = exchange(own, "xl", 1)
    beside = exchange(own, "co", 1)

    mine = lax.all_to_all(low, CHIPS, split_axis=0, concat_axis=0, tiled=True).reshape(4096, DE)
    beyond = exchange(across, "co", 1)
    mine, across, beside, beyond = lax.optimization_barrier((mine, across, beside, beyond))
    other = exchange(mine, "co", 1)
    group = [own, beside, across, beyond]
    spread, spread_t, formed = pl.pallas_call(
        form_kernel,
        out_shape=(
            jax.ShapeDtypeStruct((512, DE), bf16),
            jax.ShapeDtypeStruct((DE, 512), bf16),
            jax.ShapeDtypeStruct((PAIR_ROWS, 128, DE), bf16),
        ),
        in_specs=vmem(1) + [pl.BlockSpec(memory_space=pl.ANY)] * 4,
        out_specs=tuple(vmem(3)),
        scratch_shapes=[
            pltpu.VMEM((GROUP, 16, DE), bf16),
            pltpu.SemaphoreType.DMA((GROUP,)),
        ],
        compiler_params=pltpu.CompilerParams(vmem_limit_bytes=24 * 1024 * 1024),
        cost_estimate=pl.CostEstimate(
            flops=2 * 512 * 256 * 4096, bytes_accessed=8 * 1024 * 1024, transcendentals=0
        ),
    )(mine, *group)

    meta = jnp.concatenate(
        [jnp.stack([member, co, side]).astype(jnp.int32), partner_table.reshape(-1)]
    )
    head_now, tail_now, loss_now, pay = pl.pallas_call(
        train_kernel,
        out_shape=(
            jax.ShapeDtypeStruct((256, DE), f32),
            jax.ShapeDtypeStruct((256, DE), f32),
            jax.ShapeDtypeStruct((GROUP, 256), f32),
            jax.ShapeDtypeStruct((32, 80, DE), bf16),
        ),
        in_specs=[pl.BlockSpec(memory_space=pltpu.SMEM)]
        + vmem(1)
        + [pl.BlockSpec(memory_space=pl.ANY)]
        + vmem(2)
        + [pl.BlockSpec(memory_space=pl.ANY)] * 4
        + vmem(3),
        out_specs=tuple(vmem(4)),
        scratch_shapes=[
            pltpu.VMEM((64, 256, 256), bf16),
            pltpu.VMEM((64, 64, 256), f32),
            pltpu.VMEM((GROUP, 256, DE), f32),
            pltpu.VMEM((GROUP, 256, DE), bf16),
            pltpu.VMEM((GROUP, 64, DE), bf16),
            pltpu.VMEM((GROUP, 256, DE), f32),
            pltpu.VMEM((GROUP, 256, DE), bf16),
            pltpu.VMEM((GROUP, 2, 256, DE), bf16),
            pltpu.VMEM((GROUP, 2, 256, DE), bf16),
            pltpu.VMEM((GROUP, 2, TILE, DE), bf16),
            pltpu.VMEM((4096, DE), bf16),
            pltpu.VMEM((GROUP, 544, DE), bf16),
            pltpu.SemaphoreType.DMA((GROUP + 1,)),
        ],
        compiler_params=pltpu.CompilerParams(vmem_limit_bytes=36 * 1024 * 1024),
    )(meta, mine, other, head_vectors, tail_vectors, *group, spread, spread_t, formed)

    got = lax.all_to_all(
        pay, AXES, split_axis=0, concat_axis=0, tiled=True, axis_index_groups=near_groups()
    )
    own_grad, square, rel_part = pl.pallas_call(
        sum_kernel,
        out_shape=(
            jax.ShapeDtypeStruct((64, DE), f32),
            jax.ShapeDtypeStruct((128, 128), f32),
            jax.ShapeDtypeStruct((DR, REL_PAD), f32),
        ),
        in_specs=vmem(1),
        out_specs=tuple(vmem(3)),
        compiler_params=pltpu.CompilerParams(vmem_limit_bytes=32 * 1024 * 1024),
    )(got)
    rel_parts = [rel_part] + [exchange(rel_part, MEMBERS, s) for s in range(1, GROUP)]
    squares = lax.all_to_all(square, AXES, split_axis=0, concat_axis=0, tiled=True)
    core_updated, moment_updated, second_updated, rel_sum = pl.pallas_call(
        adam_kernel,
        out_shape=(
            jax.ShapeDtypeStruct((64, DE), f32),
            jax.ShapeDtypeStruct((64, DE), f32),
            jax.ShapeDtypeStruct((64, DE), f32),
            jax.ShapeDtypeStruct((DR, rel_count), f32),
        ),
        in_specs=vmem(9),
        out_specs=tuple(vmem(4)),
        compiler_params=pltpu.CompilerParams(vmem_limit_bytes=32 * 1024 * 1024),
    )(squares, own_grad, core_tensor, core_moment, core_second, *rel_parts)
    return (
        head_now,
        tail_now,
        loss_now.T,
        core_updated,
        moment_updated,
        second_updated,
        rel_sum.T,
    )


def solution(mesh):
    fine = Mesh(mesh.devices.reshape(2, 2, 4, 2, 4), AXES)
    rows = P(AXES, None)
    return jax.shard_map(
        body,
        mesh=fine,
        in_specs=(rows, rows, rows, rows, rows, P(), rows, rows, P(GROUPS, None, None)),
        out_specs=(rows, rows, rows, rows, rows, rows, P()),
        check_vma=False,
    )
```
